512 devices in a mesh: section: 2 (over core), seq: 64 (over y, z), mp: 4 (over x).
Axes of the slice: x: 4, y: 8, z: 8, core: 2. Of those that a mesh axis runs over, the one named last changes fastest.
Arguments:
- enc_rows: bfloat16 [2, 768, 1536], P('section', 'seq'), may hold values from -6 to 6
- vis_index: int32 [2, 768], P('section', 'seq'), may hold values from 0 to 8639, as said below
- owner_of: int32 [8640], replicated, may hold values from 0 to 63, as said below
- enc_gain: bfloat16 [1536], replicated, may hold values from 0.5 to 1.5
- embed_weight: bfloat16 [1536, 768], P('section'), may hold values from -0.15625 to 0.15625
- mask_token: bfloat16 [768], replicated, may hold values from -4 to 4
- attn_gain: bfloat16 [768], replicated, may hold values from 0.5 to 1.5
- qkv_weight: bfloat16 [768, 3, 768], P('section', None, 'mp')
- out_weight: bfloat16 [768, 768], P('mp', 'section'), may hold values from -0.21875 to 0.21875
- mlp_gain: bfloat16 [768], replicated, may hold values from 0.5 to 1.5
- up_weight: bfloat16 [768, 3072], P('section', 'mp'), may hold values from -0.21875 to 0.21875
- down_weight: bfloat16 [3072, 768], P('mp', 'section'), may hold values from -0.109375 to 0.109375
Outputs:
- decoded: float32 [2, 8640, 768], P('section', 'seq')
The draws below stay inside these ranges and needn't reach their ends.
Inputs may be any that keep to these rules, and one draw needn't show every extreme that they name: `vis_index`: each volume's row names 768 different patches. `owner_of`: each owner owns exactly 135 patches.
All inputs are finite; a program needn't handle non-finite values.
Results may differ from the reference program's by a relative error of at most 0.012.
Values may be sent and summed in bfloat16 or wider, within the bound.
A program may use at most 64 MiB of HBM per device.

```python
import jax
import jax.numpy as jnp
from jax import lax

GX = 6
P_SIZE = 8640
PAT_DEV = 135
VIS = 768
VOLS = 2
E = 1536
DD = 768
HEADS = 12
HD = 64
DFF = 3072


def draw_vis_index(key, part):
    volume_keys = jax.random.split(key, VOLS)

    def shuffled(single_key):
        return jax.random.permutation(single_key, P_SIZE)
    return jax.vmap(shuffled)(volume_keys)[:, :VIS].astype(jnp.int32)


def draw_owner_of(key, part):
    return (jax.random.permutation(key, P_SIZE) // PAT_DEV).astype(jnp.int32)


def draw_qkv_weight(key, part):
    weights_drawn = jax.random.normal(key, (DD, 3, DD), jnp.float32) * DD ** (-0.5)
    query_part = weights_drawn[:, 0, :] * 4.0
    key_part = weights_drawn[:, 1, :]
    weights_drawn = jnp.stack([query_part, key_part, weights_drawn[:, 2, :]], axis=1)
    return weights_drawn.astype(jnp.bfloat16)


def shard_levels(rng, extent, cuts, smallest, top_value):
    def one(axis_at, shards_of):
        heights = jax.random.uniform(jax.random.fold_in(jax.random.fold_in(rng, 6), axis_at), (shards_of,), jnp.float32, smallest / len(cuts), top_value / len(cuts))
        return jnp.repeat(jnp.exp(heights), extent[axis_at] // shards_of).reshape((-1,) + (1,) * (len(extent) - axis_at - 1))

    loudness = one(*cuts[0])
    for cut in cuts[1:]:
        loudness = loudness * one(*cut)
    return loudness


def normal_values(stream_key, dims, width, limit, cuts=(), kind=jnp.bfloat16):
    values = width * jax.random.normal(stream_key, dims, jnp.float32)
    if cuts:
        values = values * shard_levels(stream_key, dims, cuts, -0.22, 0.18)
    return jnp.clip(values, -limit, limit).astype(kind)


def setup_inputs(seed: int = 0) -> dict:
    splits = jax.random.split(jax.random.key(seed), 13)
    return {
        "enc_rows": normal_values(splits[0], (VOLS, VIS, E), 1.0, 6.0, ((0, 2), (1, 64))),
        "vis_index": draw_vis_index(jax.random.fold_in(splits[12], 71), 0),
        "owner_of": draw_owner_of(jax.random.fold_in(splits[12], 71), 0),
        "enc_gain": jnp.clip(1.0 + 0.1 * jax.random.normal(splits[3], (E,), jnp.float32), 0.5, 1.5).astype(jnp.bfloat16),
        "embed_weight": normal_values(splits[4], (E, DD), E ** -0.5, 0.15625, ((0, 2),)),
        "mask_token": normal_values(splits[5], (DD,), 1.0, 4.0),
        "attn_gain": jnp.clip(1.0 + 0.1 * jax.random.normal(splits[6], (DD,), jnp.float32), 0.5, 1.5).astype(jnp.bfloat16),
        "qkv_weight": draw_qkv_weight(jax.random.fold_in(splits[12], 71), 0),
        "out_weight": normal_values(splits[8], (DD, DD), DD ** -0.5, 0.21875, ((0, 4), (1, 2))),
        "mlp_gain": jnp.clip(1.0 + 0.1 * jax.random.normal(splits[9], (DD,), jnp.float32), 0.5, 1.5).astype(jnp.bfloat16),
        "up_weight": normal_values(splits[10], (DD, DFF), DD ** -0.5, 0.21875, ((0, 2), (1, 4))),
        "down_weight": normal_values(splits[11], (DFF, DD), DFF ** -0.5, 0.109375, ((0, 4), (1, 2))),
    }


def place_codes(patches, features):
    half_width = features // 8
    coordinates = jnp.stack([patches % GX, patches // GX % GX, patches // (GX * GX) % GX, patches // (GX * GX * GX)], axis=1).astype(jnp.float32)
    frequency = 1.0 / 10000.0 ** (jnp.arange(half_width, dtype=jnp.float32) / half_width)
    angles = coordinates[:, :, None] * frequency[None, None, :]
    return jnp.concatenate([jnp.sin(angles), jnp.cos(angles)], axis=2).reshape(patches.shape[0], features)

def layer_norm(values, scales):
    centred = values - lax.optimization_barrier(jnp.mean(values, axis=-1, keepdims=True))
    spread = lax.optimization_barrier(jnp.mean(centred * centred, axis=-1, keepdims=True))
    return centred * lax.rsqrt(spread + 1e-06) * scales.astype(jnp.float32)

def reference(enc_rows, vis_index, owner_of, enc_gain, embed_weight, mask_token, attn_gain, qkv_weight, out_weight, mlp_gain, up_weight, down_weight):
    owner_order = jnp.argsort(owner_of, stable=True).astype(jnp.int32)
    slot_of = jnp.zeros((P_SIZE,), jnp.int32).at[owner_order].set(jnp.arange(P_SIZE, dtype=jnp.int32))
    place_rows = place_codes(owner_order, DD)
    mask_row = mask_token.astype(jnp.float32)
    query_rows = GX * GX * GX
    outputs = []
    for volume in range(VOLS):
        normed_enc = layer_norm(enc_rows[volume].astype(jnp.float32), enc_gain).astype(jnp.bfloat16)
        embedded = jnp.dot(normed_enc, embed_weight, preferred_element_type=jnp.float32).astype(jnp.bfloat16)
        embedded = lax.optimization_barrier(embedded)
        visible_slots = slot_of[vis_index[volume]]
        start_rows = jnp.broadcast_to(mask_row[None, :], (P_SIZE, DD)).at[visible_slots].set(embedded.astype(jnp.float32))
        stream = start_rows + place_rows
        attn_in = layer_norm(stream, attn_gain).astype(jnp.bfloat16)
        projected = jnp.dot(attn_in, qkv_weight.reshape(DD, 3 * DD), preferred_element_type=jnp.float32).astype(jnp.bfloat16)
        projected = lax.optimization_barrier(projected).reshape(P_SIZE, 3, HEADS, HD)
        key_heads = projected[:, 1].astype(jnp.float32)
        value_heads = projected[:, 2].astype(jnp.float32)
        query_blocks = projected[:, 0].reshape(P_SIZE // query_rows, query_rows, HEADS, HD)

        def attend_block(query_block):
            scores = jnp.einsum('qhd,khd->hqk', query_block.astype(jnp.float32), key_heads) * HD ** (-0.5)
            row_peak = lax.optimization_barrier(jnp.max(scores, axis=-1, keepdims=True))
            exponent = jnp.exp(scores - row_peak)
            totals = lax.optimization_barrier(jnp.sum(exponent, axis=-1))
            weights = lax.optimization_barrier(exponent.astype(jnp.bfloat16))
            context = jnp.einsum('hqk,khd->hqd', weights.astype(jnp.float32), value_heads) / totals[:, :, None]
            return jnp.transpose(context, (1, 0, 2)).reshape(query_rows, DD).astype(jnp.bfloat16)
        context = lax.map(attend_block, query_blocks).reshape(P_SIZE, DD)
        middle = stream + jnp.dot(context, out_weight, preferred_element_type=jnp.float32)
        mlp_in = layer_norm(middle, mlp_gain).astype(jnp.bfloat16)
        hidden = jax.nn.gelu(jnp.dot(mlp_in, up_weight, preferred_element_type=jnp.float32), approximate=False).astype(jnp.bfloat16)
        outputs.append(middle + jnp.dot(hidden, down_weight, preferred_element_type=jnp.float32))
    return jnp.stack(outputs, axis=0)
```

```python
import functools

import jax
import jax.numpy as jnp
import numpy as np
from jax import lax
from jax.experimental import pallas as pl
from jax.experimental.pallas import tpu as pltpu
from jax.sharding import PartitionSpec as P

MESH = pl.DeviceIdType.MESH
F32 = jnp.float32
BF16 = jnp.bfloat16
GX = 6
PATCHES = 8640
OWN = 135
ROWS = 144
VIS_DEV = 12
WIDTH = 768
ENC = 1536
LOCAL = 192
HD = 64
NEG = -1e30
KEYS = 8704
CHUNK = 2176


def code_table():
    half = WIDTH // 8
    frequency = (1.0 / 10000.0 ** (np.arange(half, dtype=np.float32) / half)).astype(np.float32)
    table = np.zeros((64, WIDTH), np.float32)
    for c, (base, count) in enumerate(((0, GX), (8, GX), (16, GX), (24, 40))):
        angle = np.arange(count, dtype=np.float32)[:, None] * frequency[None, :]
        table[base : base + count, c * 192 : c * 192 + half] = np.sin(angle)
        table[base : base + count, c * 192 + half : (c + 1) * 192] = np.cos(angle)
    pieces = []
    for _ in range(3):
        piece = table.astype(BF16)
        pieces.append(piece)
        table = table - piece.astype(np.float32)
    return np.concatenate(pieces, axis=0)


def iota(shape, axis):
    return lax.broadcasted_iota(jnp.int32, shape, axis)


def fiota(shape, axis):
    return iota(shape, axis).astype(F32)


def nn(a, b):
    return lax.dot_general(a, b, (((1,), (0,)), ((), ())), preferred_element_type=F32)


def nt(a, b):
    return lax.dot_general(a, b, (((1,), (1,)), ((), ())), preferred_element_type=F32)


def coordinates(patch):
    c3 = jnp.floor((patch + 0.5) * (1.0 / 216.0))
    rest = patch - 216.0 * c3
    c2 = jnp.floor((rest + 0.5) * (1.0 / 36.0))
    rest = rest - 36.0 * c2
    c1 = jnp.floor((rest + 0.5) * (1.0 / 6.0))
    return rest - 6.0 * c1, c1, c2, c3


def one_hot_rows(patch, lanes):
    c0, c1, c2, c3 = coordinates(patch)
    lane = (iota((patch.shape[0], lanes), 1) & 63).astype(F32)
    value = jnp.where(
        lane < 8, c0, jnp.where(lane < 16, c1 + 8, jnp.where(lane < 24, c2 + 16, c3 + 24))
    )
    return jnp.where(lane == value, 1.0, 0.0).astype(BF16)


def norm(values):
    centred = values - jnp.mean(values, axis=-1, keepdims=True)
    spread = jnp.mean(centred * centred, axis=-1, keepdims=True)
    return centred * lax.rsqrt(spread + 1e-06)


def select(target, source, count):
    lane = fiota((target.shape[0], count), 1)
    return jnp.where(lane == source, 1.0, 0.0).astype(BF16)


def kernel(
    enc, vis, owner, vecs, ct3, embed_w, qkv_w, out_w, up_w, down_w,
    result,
    E2, W2, O2, U2, D2, encf, vrow, P1, P2, R1, R2, GQ, GE, GK1, GK2, IDG,
    rankf, KT, VT, XC, XE, PB, RX, YX, SC, QB, ACC, MX, LS, STREAM, MID,
    loc_sem, ws, wr, os_, or_, fs, fr, p1s, p1r, p2s, p2r,
    ids_s, ids_r, qs, qr, es, er, k1s, k1r, k2s, k2r,
    xcs, xcr, xes, xer, rss, rsr, ags, agr,
):
    s = lax.axis_index("section")
    seq = lax.axis_index("seq")
    m = lax.axis_index("mp")
    y = seq // 8
    z = seq % 8
    partner = {"section": 1 - s}

    def zdev(k):
        return {"seq": y * 8 + (z + k) % 8}

    def ydev(k):
        return {"seq": ((y + k) % 8) * 8 + z}

    def xdev(k):
        return {"mp": (m + k) % 4}

    def remote(src, dst, send, recv, device):
        return pltpu.make_async_remote_copy(
            src_ref=src, dst_ref=dst, send_sem=send, recv_sem=recv, device_id=device, device_id_type=MESH
        )

    def ring(n, first=1):
        def run(f):
            lax.fori_loop(first, n, lambda k, c: (f(k), c)[1], 0)

        return run

    def halves(ref_out, ref_in, i):
        return pltpu.make_async_copy(ref_in, ref_out.at[s], loc_sem.at[i])

    barrier = pltpu.get_barrier_semaphore()
    pl.semaphore_signal(barrier, inc=1, device_id=partner, device_id_type=MESH)
    ring(8)(lambda k: pl.semaphore_signal(barrier, inc=1, device_id=zdev(k), device_id_type=MESH))
    ring(8)(lambda k: pl.semaphore_signal(barrier, inc=1, device_id=ydev(k), device_id_type=MESH))
    ring(4)(lambda k: pl.semaphore_signal(barrier, inc=1, device_id=xdev(k), device_id_type=MESH))

    own_out = pltpu.make_async_copy(out_w, O2.at[s, m, pl.ds(0, LOCAL)], loc_sem.at[4])
    local = [halves(E2, embed_w, 0), halves(W2, qkv_w, 1), halves(U2, up_w, 2), halves(D2, down_w, 3), own_out]
    for copy in local:
        copy.start()
    pad = jnp.zeros((64, 384), BF16)
    for i in range(4):
        O2[s, i, LOCAL:256, :] = pad
    pl.semaphore_wait(barrier, 18)

    weights = [
        remote(src, dst.at[s], ws.at[i], wr.at[i], partner)
        for i, (src, dst) in enumerate(((embed_w, E2), (qkv_w, W2), (up_w, U2), (down_w, D2)))
    ]
    weights[0].start()
    weights[1].start()

    def out_copy(k):
        return remote(out_w, O2.at[s, m, pl.ds(0, LOCAL)], os_.at[k], or_.at[k], xdev(k))

    ring(4)(lambda k: out_copy(k).start())

    mask_row = vecs[0:1, :]
    attn_gain = vecs[1:2, :]
    mlp_gain = vecs[2:3, :]
    enc_gain = jnp.concatenate([vecs[3:4, :], vecs[4:5, :]], axis=1)
    table = ct3[...]
    vrow[...] = jnp.full((8, 128), -1.0, F32)
    vrow[0:1, 0:VIS_DEV] = vis[...].astype(F32)
    vids = vrow[0:1, :]
    vcol = jnp.sum(
        jnp.where(iota((16, 128), 1) == iota((16, 128), 0), jnp.broadcast_to(vids, (16, 128)), 0.0),
        axis=1, keepdims=True,
    )
    vis_code = nn(one_hot_rows(jnp.maximum(vcol, 0.0), 192), table)
    encf[...] = jnp.zeros((16, ENC), F32)
    encf[0:VIS_DEV, :] = enc[0].astype(F32)
    normed = (norm(encf[...]) * enc_gain).astype(BF16)

    flags = jnp.where(owner[...] == seq, 1.0, 0.0).astype(F32)
    flagb = flags.astype(BF16)
    upper = jnp.where(iota((128, 128), 0) <= iota((128, 128), 1), 1.0, 0.0).astype(BF16)
    lower = jnp.where(iota((72, 72), 1) < iota((72, 72), 0), 1.0, 0.0).astype(BF16)
    within = nn(flagb, upper)
    before = jnp.sum(nn(lower, flagb), axis=1, keepdims=True)
    rankf[...] = jnp.where(flags > 0.5, within + before - 1.0, -1.0)
    own_j = fiota((ROWS, 128), 0)
    lane_row = fiota((ROWS, 128), 1)

    def find(h, total):
        row = jnp.broadcast_to(rankf[pl.ds(h, 1), :], (ROWS, 128))
        return total + jnp.where(row == own_j, lane_row + (h * 128).astype(F32), 0.0)

    own_ids = jnp.sum(
        lax.fori_loop(0, 68, find, jnp.zeros((ROWS, 128), F32), unroll=4), axis=1, keepdims=True
    )
    own_code = nn(one_hot_rows(own_ids, 192), table)

    row64 = iota((64, WIDTH), 0)
    lane64 = iota((64, WIDTH), 1)
    group = jnp.where(row64 < 8, 0, jnp.where(row64 < 16, 1, jnp.where(row64 < 24, 2, 3)))
    inside = (lane64 >= group * 192) & (lane64 < group * 192 + 192)
    mask_centred = mask_row - jnp.mean(mask_row, axis=-1, keepdims=True)
    code = table[0:64].astype(F32) + table[64:128].astype(F32) + table[128:192].astype(F32)
    block = jnp.where(inside, mask_centred + code, 0.0)
    block_sum = jnp.sum(block, axis=1, keepdims=True)
    block_mean = block_sum * (1.0 / 192.0)
    off = jnp.where(inside, block - block_mean, 0.0)
    spread = jnp.sum(off * off, axis=1, keepdims=True)
    scaled = (block - block_sum * (1.0 / 768.0)) * attn_gain
    scaled_hi = scaled.astype(BF16)
    scaled_lo = (scaled - scaled_hi.astype(F32)).astype(BF16)
    pieces = jnp.concatenate([scaled_hi, scaled_lo], axis=0)
    lane128 = iota((64, 128), 1)
    row128 = iota((64, 128), 0)
    group128 = jnp.where(row128 < 8, 0, jnp.where(row128 < 16, 1, jnp.where(row128 < 24, 2, 3)))
    stat = jnp.where(lane128 == group128, block_mean, 0.0) + jnp.where(lane128 == 4, spread, 0.0)
    stat_t = jnp.transpose(jnp.concatenate([stat, stat], axis=0))[0:16, :]

    local[0].wait()
    weights[0].wait_recv()
    embedded = (nn(normed[:, 0:WIDTH], E2[0]) + nn(normed[:, WIDTH:ENC], E2[1])).astype(BF16)
    attn_vis = (norm(embedded.astype(F32) + vis_code) * attn_gain).astype(BF16)
    local[1].wait()
    weights[1].wait_recv()
    qk = nt(attn_vis[:, 0:384], W2[0, 0:384, :]) + nt(attn_vis[:, 384:768], W2[1, 0:384, :])
    kv = nt(attn_vis[:, 0:384], W2[0, LOCAL:576, :]) + nt(attn_vis[:, 384:768], W2[1, LOCAL:576, :])
    lane16 = iota((16, 384), 1)
    row16 = fiota((16, 1), 0)

    def pick(low, high, shift):
        return select(row16, jnp.where((row16 >= low) & (row16 < high), row16 + shift, -1.0), 16)

    first, second, third = pick(0, 6, 0), pick(0, 6, 6), pick(6, 12, -6)

    def pack(pair, keys_values):
        left = jnp.where(lane16 < LOCAL, pair, 0.0).astype(BF16)
        right = jnp.where(lane16 >= LOCAL, pltpu.roll(pair, LOCAL, 1), 0.0).astype(BF16)
        return nn(first, left) + nn(second, right) + nn(keys_values, kv.astype(BF16))

    vhi = jnp.floor((vids + 0.5) * (1.0 / 128.0))
    vlo = vids - 128.0 * vhi
    row_ids = iota((16, 128), 0)
    id_part = jnp.where(row_ids == 12, vhi, jnp.where(row_ids == 13, vlo, 0.0))
    id_part = jnp.concatenate([id_part, jnp.zeros((16, 256), F32)], axis=1)
    P1[...] = (pack(qk, third) + id_part).astype(BF16)
    quarter = pltpu.roll(embedded.astype(F32), (WIDTH - m * LOCAL) % WIDTH, 1)[:, 0:384]
    P2[...] = pack(quarter, pick(6, 12, 0)).astype(BF16)
    R1[z] = P1[...]
    R2[y] = P2[...]

    def p1_copy(k):
        return remote(P1, R1.at[z], p1s.at[k], p1r.at[k], zdev(k))

    def p2_copy(k):
        return remote(P2, R2.at[y], p2s.at[k], p2r.at[k], ydev(k))

    ring(8)(lambda k: (p1_copy(k).start(), p2_copy(k).start()))
    weights[2].start()
    weights[3].start()

    kv_w0, kv_w1 = W2[0, LOCAL:576, :], W2[1, LOCAL:576, :]
    proj = nt(kv_w0, pieces[:, 0:384]) + nt(kv_w1, pieces[:, 384:768])
    proj = proj + pltpu.roll(proj, 64, 1)
    proj_hi = proj.astype(BF16)
    lane_p = iota((384, 128), 1)
    kv_table = jnp.where(lane_p < 64, proj_hi.astype(F32), proj - proj_hi.astype(F32)).astype(BF16)
    stat_hi = stat_t.astype(BF16)
    stat_table = jnp.where(
        iota((16, 128), 1) < 64, stat_hi.astype(F32), stat_t - stat_hi.astype(F32)
    ).astype(BF16)
    big_table = jnp.concatenate([kv_table, stat_table], axis=0)

    stream0 = mask_row + own_code
    attn_own = (norm(stream0) * attn_gain).astype(BF16)
    q_masked = nt(attn_own[:, 0:384], W2[0, 0:256, :]) + nt(attn_own[:, 384:768], W2[1, 0:256, :])

    def build(c):
        width = 512
        start = pl.multiple_of(c * width, width)
        patch = (iota((1, width), 1) + start).astype(F32)
        c0, c1, c2, c3 = coordinates(patch)
        sub = fiota((64, width), 0)
        value = jnp.where(
            sub < 8, c0, jnp.where(sub < 16, c1 + 8, jnp.where(sub < 24, c2 + 16, c3 + 24))
        )
        hot = jnp.where(sub == value, 1.0, 0.0).astype(BF16)
        raw = nn(big_table, jnp.concatenate([hot, hot], axis=0))
        m0, m1, m2, m3 = raw[384:385], raw[385:386], raw[386:387], raw[387:388]
        mean = (m0 + m1 + m2 + m3) * 0.25
        between = (m0 - mean) ** 2 + (m1 - mean) ** 2 + (m2 - mean) ** 2 + (m3 - mean) ** 2
        scale = lax.rsqrt(raw[388:389] * (1.0 / 768.0) + between * 0.25 + 1e-06)
        KT[0:LOCAL, pl.ds(start, width)] = (raw[0:LOCAL] * scale).astype(BF16)
        VT[0:LOCAL, pl.ds(start, width)] = (raw[LOCAL:384] * scale).astype(BF16)
        KT[LOCAL:256, pl.ds(start, width)] = jnp.zeros((64, width), BF16)
        VT[LOCAL:256, pl.ds(start, width)] = jnp.zeros((64, width), BF16)

    lax.fori_loop(0, 6, lambda c, x: (build(c), x)[1], 0)

    def wait_in(copies, n, slot, ref, sem):
        def one(k, c):
            remote(ref.at[slot(k)], ref.at[slot(k)], sem.at[k], sem.at[k], partner).wait_recv()
            return c

        lax.fori_loop(1, n, one, 0)

    def from_z(k):
        return (z + 8 - k) % 8

    def from_y(k):
        return (y + 8 - k) % 8

    def from_x(k):
        return (m + 4 - k) % 4

    wait_in(None, 8, from_z, R1, p1r)
    wait_in(None, 8, from_y, R2, p2r)
    col = fiota((112, 1), 0)
    small = jnp.where(col < 48, col, col - 48)
    src = jnp.floor((small + 0.5) * (1.0 / 6.0))
    src = 16.0 * src + (small - 6.0 * src) + jnp.where(col < 48, 0.0, 6.0)
    src = jnp.where(col < 96, src, jnp.where(col < 104, 16.0 * (col - 96) + 12, 16.0 * (col - 104) + 13))
    chooser = select(col, src, 128)
    got1 = nn(chooser, R1[...].reshape(128, 384))
    got2 = nn(chooser[0:96], R2[...].reshape(128, 384))
    GQ[y] = got1[0:48].astype(BF16)
    GK1[y] = got1[48:96].astype(BF16)
    IDG[y] = 128.0 * got1[96:104, 0:128] + got1[104:112, 0:128]
    GE[z] = got2[0:48].astype(BF16)
    GK2[z] = got2[48:96].astype(BF16)

    def over(ref, slot, send, recv, device):
        def copy(k):
            return remote(ref.at[slot], ref.at[slot], send.at[k], recv.at[k], device(k))

        return copy

    c_ids = over(IDG, y, ids_s, ids_r, ydev)
    c_q = over(GQ, y, qs, qr, ydev)
    c_e = over(GE, z, es, er, zdev)
    c_k1 = over(GK1, y, k1s, k1r, ydev)
    c_k2 = over(GK2, z, k2s, k2r, zdev)
    ring(8)(lambda k: (c_ids(k).start(), c_q(k).start(), c_e(k).start()))
    ring(8)(lambda k: (c_k1(k).start(), c_k2(k).start()))

    local[4].wait()
    wait_in(None, 4, lambda k: (s, from_x(k), pl.ds(0, LOCAL)), O2, or_)
    forward = remote(O2.at[s], O2.at[s], fs.at[0], fr.at[0], partner)
    forward.start()

    lax.fori_loop(6, 17, lambda c, x: (build(c), x)[1], 0)

    wait_in(None, 8, from_y, IDG, ids_r)
    ids = IDG[...].reshape(64, 128)
    lane_i = fiota((64, 128), 1)
    source = fiota((64, 1), 0) + 1.0
    hots, where_d, where_i = [], [], []
    for i in range(VIS_DEV):
        one = ids[:, i : i + 1]
        high = jnp.floor((one + 0.5) * (1.0 / 128.0))
        low = one - 128.0 * high
        hots.append(jnp.where(lane_i == high, 1.0, 0.0))
        hot = jnp.where(lane_i == low, 1.0, 0.0)
        where_d.append((hot * source).astype(BF16))
        where_i.append((hot * float(i)).astype(BF16))
    hot_t = jnp.transpose(jnp.concatenate(hots, axis=0)).astype(BF16)
    found = nn(
        hot_t,
        jnp.concatenate(
            [jnp.concatenate(where_d, axis=0), jnp.concatenate(where_i, axis=0)], axis=1
        ),
    )
    seen = found[:, 0:128]
    patch2 = fiota((128, 128), 0) * 128.0 + fiota((128, 128), 1)
    bias = jnp.where((seen > 0.5) | (patch2 >= PATCHES), NEG, 0.0)
    sub16 = iota((16, 128), 0)
    for h in range(68):
        KT[LOCAL : LOCAL + 16, h * 128 : (h + 1) * 128] = jnp.where(
            sub16 == 0, jnp.broadcast_to(bias[h : h + 1, :], (16, 128)), 0.0
        ).astype(BF16)
    own_hi = jnp.floor((own_ids + 0.5) * (1.0 / 128.0))
    own_lo = own_ids - 128.0 * own_hi
    hit_hi = jnp.where(lane_row == own_hi, 1.0, 0.0).astype(BF16)
    hit_lo = lane_row == own_lo
    place = nn(hit_hi, found.astype(BF16))
    own_d = jnp.sum(jnp.where(hit_lo, place[:, 0:128], 0.0), axis=1, keepdims=True) - 1.0
    own_i = jnp.sum(jnp.where(hit_lo, place[:, 128:256], 0.0), axis=1, keepdims=True)
    is_vis = own_d > -0.5
    late = own_i > 5.5
    own_i6 = jnp.where(late, own_i - 6.0, own_i)
    own_y = jnp.floor((own_d + 0.5) * 0.125)
    own_z = own_d - 8.0 * own_y
    row_yz = own_y * 48.0 + own_z * 6.0 + own_i6
    row_zy = own_z * 48.0 + own_y * 6.0 + own_i6

    def choose(row, gathered):
        lane = fiota((ROWS, 384), 1)
        hit = jnp.where((lane == row) & is_vis, 1.0, 0.0)
        one = nn(jnp.where(late, 0.0, hit).astype(BF16), gathered)
        two = nn(jnp.where(late, hit, 0.0).astype(BF16), gathered)
        both = one + pltpu.roll(two, LOCAL, 1)
        return jnp.where(iota((ROWS, 256), 1) < LOCAL, both[:, 0:256], 0.0)

    wait_in(None, 8, from_y, GQ, qr)
    q_vis = choose(row_yz, GQ[...].reshape(384, 384))
    queries = jnp.where(is_vis, q_vis, q_masked).astype(BF16).astype(F32) * (HD ** -0.5)
    lane_q = iota((ROWS, 256), 1)
    for h in range(3):
        keep = (lane_q >= h * HD) & (lane_q < (h + 1) * HD)
        QB[h * ROWS : (h + 1) * ROWS, :] = jnp.where(
            keep, queries, jnp.where(lane_q == LOCAL, 1.0, 0.0)
        ).astype(BF16)

    wait_in(None, 8, from_z, GE, er)
    XE[m] = choose(row_zy, GE[...].reshape(384, 384)).astype(BF16)

    c_xe = over(XE, m, xes, xer, xdev)
    ring(4)(lambda k: c_xe(k).start())

    MX[...] = jnp.full((3 * ROWS, 128), NEG, F32)
    LS[...] = jnp.zeros((3 * ROWS, 128), F32)
    ACC[...] = jnp.zeros((3 * ROWS, 256), F32)

    def absorb(scores, width, product):
        peak_old = MX[...]
        peak = jnp.maximum(peak_old, jnp.max(scores, axis=1, keepdims=True))
        factor = jnp.exp(peak_old - peak)
        weights_ = jnp.exp(scores - peak[:, 0:1])
        total = weights_[:, 0:128]
        for t in range(1, width // 128):
            total = total + weights_[:, t * 128 : (t + 1) * 128]
        MX[...] = peak
        LS[...] = LS[...] * factor + total
        ACC[...] = ACC[...] * jnp.concatenate([factor, factor], axis=1) + product(weights_.astype(BF16))

    def masked(c, x):
        start = pl.multiple_of(c * CHUNK, 128)
        scores = nn(QB[...], KT[:, pl.ds(start, CHUNK)])
        absorb(scores, CHUNK, lambda w: nt(w, VT[:, pl.ds(start, CHUNK)]))
        return x

    lax.fori_loop(0, KEYS // CHUNK, masked, 0)

    wait_in(None, 8, from_y, GK1, k1r)
    wait_in(None, 8, from_z, GK2, k2r)
    q_only = jnp.where(iota((3 * ROWS, 256), 1) < LOCAL, QB[...].astype(F32), 0.0).astype(BF16)

    def visible(gathered):
        scores = nt(q_only, gathered[:, 0:256])
        absorb(scores, 384, lambda w: pltpu.roll(nn(w, gathered), LOCAL, 1)[:, 0:256])

    visible(GK1[...].reshape(384, 384))
    visible(GK2[...].reshape(384, 384))

    context = jnp.zeros((ROWS, 256), F32)
    for h in range(3):
        keep = (lane_q >= h * HD) & (lane_q < (h + 1) * HD)
        part = slice(h * ROWS, (h + 1) * ROWS)
        total = jnp.sum(LS[part, :], axis=1, keepdims=True)
        context = context + jnp.where(keep, ACC[part, :] / total, 0.0)
    XC[m] = context.astype(BF16)
    c_xc = over(XC, m, xcs, xcr, xdev)
    ring(4)(lambda k: c_xc(k).start())

    wait_in(None, 4, from_x, XE, xer)
    filled = jnp.zeros((ROWS, WIDTH), F32)
    for i in range(4):
        wide = jnp.concatenate([XE[i].astype(F32), jnp.zeros((ROWS, 512), F32)], axis=1)
        filled = filled + (pltpu.roll(wide, i * LOCAL, 1) if i else wide)
    stream = jnp.where(is_vis, filled, mask_row) + own_code
    STREAM[...] = stream

    local[2].wait()
    local[3].wait()
    weights[2].wait_recv()
    weights[3].wait_recv()
    forward.wait_recv()
    wait_in(None, 4, from_x, XC, xcr)
    gathered = jnp.concatenate([XC[i] for i in range(4)], axis=1)
    for half in range(2):
        cols = slice(half * 384, (half + 1) * 384)
        MID[:, cols] = STREAM[:, cols] + nn(gathered, O2[half].reshape(1024, 384))

    mlp_in = (norm(MID[...]) * mlp_gain).astype(BF16)
    raised = nn(mlp_in[:, 0:384], U2[0]) + nn(mlp_in[:, 384:768], U2[1])
    hidden = (0.5 * raised * (1.0 + lax.erf(raised * np.float32(np.sqrt(0.5))))).astype(BF16)
    for half in range(2):
        PB[half] = nn(hidden, D2[half]).astype(BF16)

    def quadrant(q):
        return PB.at[q % 2, pl.ds(pl.multiple_of((q // 2) * 64, 16), 80)]

    def rs_copy(k):
        return remote(quadrant((m + k) % 4), RX.at[m], rss.at[k], rsr.at[k], xdev(k))

    ring(4)(lambda k: rs_copy(k).start())
    RX[m] = PB[m % 2, pl.ds(pl.multiple_of((m // 2) * 64, 16), 80), :]
    wait_in(None, 4, from_x, RX, rsr)
    YX[m] = (
        RX[0].astype(F32) + RX[1].astype(F32) + RX[2].astype(F32) + RX[3].astype(F32)
    ).astype(BF16)
    c_ag = over(YX, m, ags, agr, xdev)
    ring(4)(lambda k: c_ag(k).start())
    wait_in(None, 4, from_x, YX, agr)
    for half in range(2):
        cols = slice(half * 384, (half + 1) * 384)
        result[0:80, cols] = MID[0:80, cols] + YX[half].astype(F32)
        result[80:OWN, cols] = MID[80:OWN, cols] + YX[2 + half].astype(F32)[16:71]

    for copy in weights:
        copy.wait_send()
    forward.wait_send()
    ring(4)(lambda k: (out_copy(k).wait_send(), c_xe(k).wait_send(), c_xc(k).wait_send()))
    ring(4)(lambda k: (rs_copy(k).wait_send(), c_ag(k).wait_send()))
    ring(8)(lambda k: (p1_copy(k).wait_send(), p2_copy(k).wait_send(), c_ids(k).wait_send()))
    ring(8)(lambda k: (c_q(k).wait_send(), c_e(k).wait_send(), c_k1(k).wait_send(), c_k2(k).wait_send()))


def shards(
    enc_rows, vis_index, owner_of, enc_gain, embed_weight, mask_token, attn_gain, qkv_weight,
    out_weight, mlp_gain, up_weight, down_weight,
):
    owner = jnp.pad(owner_of, (0, 72 * 128 - PATCHES), constant_values=-1).reshape(72, 128)
    vecs = jnp.stack(
        [mask_token, attn_gain, mlp_gain, enc_gain[:WIDTH], enc_gain[WIDTH:]], axis=0
    ).astype(F32)
    qkv_t = jnp.transpose(qkv_weight, (1, 2, 0)).reshape(576, 384)
    vm = pl.BlockSpec(memory_space=pltpu.VMEM)
    hbm = pl.BlockSpec(memory_space=pl.ANY)
    dma = pltpu.SemaphoreType.DMA
    V = pltpu.VMEM
    scratch = [
        V((2, 768, 768), BF16), V((2, 576, 384), BF16), V((2, 4, 256, 384), BF16),
        V((2, 384, 768), BF16), V((2, 768, 384), BF16),
        V((16, ENC), F32), V((8, 128), F32), V((16, 384), BF16), V((16, 384), BF16),
        V((8, 16, 384), BF16), V((8, 16, 384), BF16),
        V((8, 48, 384), BF16), V((8, 48, 384), BF16), V((8, 48, 384), BF16), V((8, 48, 384), BF16),
        V((8, 8, 128), F32), V((72, 128), F32),
        V((256, KEYS), BF16), V((256, KEYS), BF16),
        V((4, ROWS, 256), BF16), V((4, ROWS, 256), BF16),
        V((2, ROWS, 384), BF16), V((4, 80, 384), BF16), V((4, 80, 384), BF16),
        V((8, 128), F32), V((3 * ROWS, 256), BF16), V((3 * ROWS, 256), F32),
        V((3 * ROWS, 128), F32), V((3 * ROWS, 128), F32), V((ROWS, WIDTH), F32), V((ROWS, WIDTH), F32),
        dma((5,)), dma((4,)), dma((4,)), dma((4,)), dma((4,)), dma((1,)), dma((1,)),
    ] + [dma((8,))] * 14 + [dma((4,))] * 8
    decoded = pl.pallas_call(
        kernel,
        out_shape=jax.ShapeDtypeStruct((OWN, WIDTH), F32),
        in_specs=[vm, vm, vm, vm, vm, hbm, hbm, hbm, hbm, hbm],
        out_specs=vm,
        scratch_shapes=scratch,
        compiler_params=pltpu.CompilerParams(
            collective_id=0, has_side_effects=True, vmem_limit_bytes=56 * 1024 * 1024
        ),
        cost_estimate=pl.CostEstimate(flops=6_000_000_000, bytes_accessed=5_000_000, transcendentals=4_000_000),
    )(enc_rows, vis_index, owner, vecs, jnp.asarray(code_table()), embed_weight, qkv_t, out_weight, up_weight, down_weight)
    return decoded[None]


def solution(mesh):
    in_specs = (
        P("section", "seq", None),
        P("section", "seq"),
        P(),
        P(),
        P("section", None),
        P(),
        P(),
        P("section", None, "mp"),
        P("mp", "section"),
        P(),
        P("section", "mp"),
        P("mp", "section"),
    )
    out_specs = P("section", "seq", None)
    return jax.shard_map(shards, mesh=mesh, in_specs=in_specs, out_specs=out_specs, check_vma=False)
```

```python
import functools

import jax
import jax.numpy as jnp
import numpy as np
from jax import lax
from jax.experimental import pallas as pl
from jax.experimental.pallas import tpu as pltpu
from jax.sharding import PartitionSpec as P

MESH = pl.DeviceIdType.MESH
F32 = jnp.float32
BF16 = jnp.bfloat16
GX = 6
PATCHES = 8640
OWN = 135
ROWS = 144
VIS_DEV = 12
WIDTH = 768
ENC = 1536
LOCAL = 192
HD = 64
NEG = -1e30
KEYS = 8704
CHUNK = 2176


def code_table():
    half = WIDTH // 8
    frequency = (1.0 / 10000.0 ** (np.arange(half, dtype=np.float32) / half)).astype(np.float32)
    table = np.zeros((64, WIDTH), np.float32)
    for c, (base, count) in enumerate(((0, GX), (8, GX), (16, GX), (24, 40))):
        angle = np.arange(count, dtype=np.float32)[:, None] * frequency[None, :]
        table[base : base + count, c * 192 : c * 192 + half] = np.sin(angle)
        table[base : base + count, c * 192 + half : (c + 1) * 192] = np.cos(angle)
    pieces = []
    for _ in range(3):
        piece = table.astype(BF16)
        pieces.append(piece)
        table = table - piece.astype(np.float32)
    return np.concatenate(pieces, axis=0)


def iota(shape, axis):
    return lax.broadcasted_iota(jnp.int32, shape, axis)


def fiota(shape, axis):
    return iota(shape, axis).astype(F32)


def nn(a, b):
    return lax.dot_general(a, b, (((1,), (0,)), ((), ())), preferred_element_type=F32)


def nt(a, b):
    return lax.dot_general(a, b, (((1,), (1,)), ((), ())), preferred_element_type=F32)


def coordinates(patch):
    c3 = jnp.floor((patch + 0.5) * (1.0 / 216.0))
    rest = patch - 216.0 * c3
    c2 = jnp.floor((rest + 0.5) * (1.0 / 36.0))
    rest = rest - 36.0 * c2
    c1 = jnp.floor((rest + 0.5) * (1.0 / 6.0))
    return rest - 6.0 * c1, c1, c2, c3


def one_hot_rows(patch, lanes):
    c0, c1, c2, c3 = coordinates(patch)
    lane = (iota((patch.shape[0], lanes), 1) & 63).astype(F32)
    value = jnp.where(
        lane < 8, c0, jnp.where(lane < 16, c1 + 8, jnp.where(lane < 24, c2 + 16, c3 + 24))
    )
    return jnp.where(lane == value, 1.0, 0.0).astype(BF16)


def norm(values):
    centred = values - jnp.mean(values, axis=-1, keepdims=True)
    spread = jnp.mean(centred * centred, axis=-1, keepdims=True)
    return centred * lax.rsqrt(spread + 1e-06)


def select(target, source, count):
    lane = fiota((target.shape[0], count), 1)
    return jnp.where(lane == source, 1.0, 0.0).astype(BF16)


def kernel(
    enc, vis, owner, enc_g, mask_t, attn_g, mlp_g, ct3, embed_w, qkv_w, out_w, up_w, down_w,
    result,
    E2, W2, OA, OB, U2, D2, own2, encf, vrow, P1, P2, R1, R2, GQ, GE, GK1, GK2, IDG,
    rankf, KT, VT, XC, XE, PB, RX, YX, SC, QB, ACC, MX, LS, STREAM, MID,
    loc_sem, ws, wr, os_, or_, os2, or2, fs, fr, p1s, p1r, p2s, p2r,
    ids_ps, ids_pr, ids_ms, ids_mr, q_ps, q_pr, q_ms, q_mr, e_ps, e_pr, e_ms, e_mr,
    k1_ps, k1_pr, k1_ms, k1_mr, k2_ps, k2_pr, k2_ms, k2_mr,
    xcs, xcr, xes, xer, rss, rsr, ags, agr,
):
    s = lax.axis_index("section")
    seq = lax.axis_index("seq")
    m = lax.axis_index("mp")
    y = seq // 8
    z = seq % 8
    partner = {"section": 1 - s}

    def zdev(k):
        return {"seq": y * 8 + (z + k) % 8}

    def ydev(k):
        return {"seq": ((y + k) % 8) * 8 + z}

    def xdev(k):
        return {"mp": (m + k) % 4}

    def remote(src, dst, send, recv, device):
        return pltpu.make_async_remote_copy(
            src_ref=src, dst_ref=dst, send_sem=send, recv_sem=recv, device_id=device, device_id_type=MESH
        )

    def ring(n, first=1):
        def run(f):
            lax.fori_loop(first, n, lambda k, c: (f(k), c)[1], 0)

        return run

    groups = []

    class Group:
        def __init__(self, copy, n, slot, ref, recv):
            self.copy, self.n, self.slot, self.ref, self.sem = copy, n, slot, ref, recv
            self.waited = False
            groups.append(self)
            ring(n)(lambda k: copy(k).start())

        def wait_one(self, k):
            there = self.ref.at[self.slot(k)]
            remote(there, there, self.sem.at[k], self.sem.at[k], partner).wait_recv()

        def wait(self):
            self.waited = True
            ring(self.n)(self.wait_one)

        def left(self):
            ring(self.n)(lambda k: self.copy(k).wait_send())

    class Single:
        def __init__(self, copy):
            self.copy = copy
            self.waited = False
            groups.append(self)
            copy.start()

        def wait(self):
            self.waited = True
            self.copy.wait_recv()

        def left(self):
            self.copy.wait_send()

    class Ring:
        def __init__(self, ref, me, device, plus, sems):
            self.ref, self.me, self.device, self.plus, self.minus = ref, me, device, plus, 7 - plus
            self.ps, self.pr, self.ms, self.mr = sems
            self.waited = False
            groups.append(self)
            self.up(1).start()
            self.down(1).start()

        def up(self, t):
            block = self.ref.at[(self.me + 9 - t) % 8]
            return remote(block, block, self.ps.at[t], self.pr.at[t], self.device(1))

        def down(self, t):
            block = self.ref.at[(self.me + t - 1) % 8]
            return remote(block, block, self.ms.at[t], self.mr.at[t], self.device(7))

        def hop(self, t):
            def receive(block, sem):
                there = self.ref.at[block]
                remote(there, there, sem.at[t], sem.at[t], partner).wait_recv()

            def guard(condition, f):
                if isinstance(t, int):
                    if condition:
                        f()
                else:
                    pl.when(condition)(f)

            guard(t <= self.plus, lambda: receive((self.me + 8 - t) % 8, self.pr))
            guard(t < self.plus, lambda: self.up(t + 1).start())
            guard(t <= self.minus, lambda: receive((self.me + t) % 8, self.mr))
            guard(t < self.minus, lambda: self.down(t + 1).start())
            if isinstance(t, int) and t == 4:
                self.waited = True

        def wait(self):
            for t in range(1, 5):
                self.hop(t)

        def left(self):
            ring(self.plus + 1)(lambda t: self.up(t).wait_send())
            ring(self.minus + 1)(lambda t: self.down(t).wait_send())

    class Local:
        def __init__(self, copy):
            self.copy = copy
            self.waited = False
            groups.append(self)
            copy.start()

        def wait(self):
            self.waited = True
            self.copy.wait()

        def left(self):
            pass

    def finish():
        for g in groups:
            if not g.waited:
                g.wait()
            g.left()

    def from_z(k):
        return (z + 8 - k) % 8

    def from_y(k):
        return (y + 8 - k) % 8

    def from_x(k):
        return (m + 4 - k) % 4

    def halves(ref_out, ref_in, i):
        return pltpu.make_async_copy(ref_in, ref_out.at[s], loc_sem.at[i])

    barrier = pltpu.get_barrier_semaphore()
    pl.semaphore_signal(barrier, inc=1, device_id=partner, device_id_type=MESH)
    ring(8)(lambda k: pl.semaphore_signal(barrier, inc=1, device_id=zdev(k), device_id_type=MESH))
    ring(8)(lambda k: pl.semaphore_signal(barrier, inc=1, device_id=ydev(k), device_id_type=MESH))
    ring(4)(lambda k: pl.semaphore_signal(barrier, inc=1, device_id=xdev(k), device_id_type=MESH))

    local = [
        Local(copy)
        for copy in (
            halves(E2, embed_w, 0), halves(W2, qkv_w, 1), halves(U2, up_w, 2), halves(D2, down_w, 3),
            pltpu.make_async_copy(out_w.at[pl.ds(HD, 128)], OA.at[s, m], loc_sem.at[4]),
            pltpu.make_async_copy(out_w.at[pl.ds(0, HD)], OB.at[s, m], loc_sem.at[5]),
        )
    ]

    mask_row = mask_t[...].astype(F32).reshape(1, WIDTH)
    attn_gain = attn_g[...].astype(F32).reshape(1, WIDTH)
    mlp_gain = mlp_g[...].astype(F32).reshape(1, WIDTH)
    enc_gain = jnp.concatenate(
        [enc_g[0:WIDTH].astype(F32).reshape(1, WIDTH), enc_g[WIDTH:ENC].astype(F32).reshape(1, WIDTH)], axis=1
    )
    table = ct3[...]
    vrow[...] = jnp.full((8, 128), -1.0, F32)
    vrow[0:1, 0:VIS_DEV] = vis[...].astype(F32)
    vids = vrow[0:1, :]
    vcol = jnp.sum(
        jnp.where(iota((16, 128), 1) == iota((16, 128), 0), jnp.broadcast_to(vids, (16, 128)), 0.0),
        axis=1, keepdims=True,
    )
    vis_code = nn(one_hot_rows(jnp.maximum(vcol, 0.0), 192), table)
    encf[...] = jnp.zeros((16, ENC), F32)
    encf[0:VIS_DEV, :] = enc[0].astype(F32)
    normed = (norm(encf[...]) * enc_gain).astype(BF16)

    own2[...] = jnp.full((72, 128), -1, jnp.int32)
    for i in range(8):
        own2[i * 8 : (i + 1) * 8, :] = owner[i * 1024 : (i + 1) * 1024].reshape(8, 128)
    for i in range(64, 67):
        own2[i : i + 1, :] = owner[i * 128 : (i + 1) * 128].reshape(1, 128)
    own2[67:68, 0:64] = owner[67 * 128 : PATCHES].reshape(1, 64)
    flags = jnp.where(own2[...] == seq, 1.0, 0.0).astype(F32)
    flagb = flags.astype(BF16)
    upper = jnp.where(iota((128, 128), 0) <= iota((128, 128), 1), 1.0, 0.0).astype(BF16)
    lower = jnp.where(iota((72, 72), 1) < iota((72, 72), 0), 1.0, 0.0).astype(BF16)
    within = nn(flagb, upper)
    before = jnp.sum(nn(lower, flagb), axis=1, keepdims=True)
    rankf[...] = jnp.where(flags > 0.5, within + before - 1.0, -1.0)
    own_j = fiota((ROWS, 128), 0)
    lane_row = fiota((ROWS, 128), 1)

    def find(h, total):
        row = jnp.broadcast_to(rankf[pl.ds(h, 1), :], (ROWS, 128))
        return total + jnp.where(row == own_j, lane_row + (h * 128).astype(F32), 0.0)

    own_ids = jnp.sum(
        lax.fori_loop(0, 68, find, jnp.zeros((ROWS, 128), F32), unroll=4), axis=1, keepdims=True
    )
    pl.semaphore_wait(barrier, 18)

    def weight(i, src, dst):
        return Single(remote(src, dst.at[s], ws.at[i], wr.at[i], partner))

    g_embed = weight(0, embed_w, E2)
    g_qkv = weight(1, qkv_w, W2)

    def oa_copy(k):
        return remote(out_w.at[pl.ds(HD, 128)], OA.at[s, m], os_.at[k], or_.at[k], xdev(k))

    def ob_copy(k):
        return remote(out_w.at[pl.ds(0, HD)], OB.at[s, m], os2.at[k], or2.at[k], xdev(k))

    g_oa = Group(oa_copy, 4, lambda k: (s, from_x(k)), OA, or_)
    g_ob = Group(ob_copy, 4, lambda k: (s, from_x(k)), OB, or2)
    own_code = nn(one_hot_rows(own_ids, 192), table)

    row64 = iota((64, WIDTH), 0)
    lane64 = iota((64, WIDTH), 1)
    group = jnp.where(row64 < 8, 0, jnp.where(row64 < 16, 1, jnp.where(row64 < 24, 2, 3)))
    inside = (lane64 >= group * 192) & (lane64 < group * 192 + 192)
    mask_centred = mask_row - jnp.mean(mask_row, axis=-1, keepdims=True)
    code = table[0:64].astype(F32) + table[64:128].astype(F32) + table[128:192].astype(F32)
    block = jnp.where(inside, mask_centred + code, 0.0)
    block_sum = jnp.sum(block, axis=1, keepdims=True)
    block_mean = block_sum * (1.0 / 192.0)
    off = jnp.where(inside, block - block_mean, 0.0)
    spread = jnp.sum(off * off, axis=1, keepdims=True)
    scaled = (block - block_sum * (1.0 / 768.0)) * attn_gain
    scaled_hi = scaled.astype(BF16)
    scaled_lo = (scaled - scaled_hi.astype(F32)).astype(BF16)
    pieces = jnp.concatenate([scaled_hi, scaled_lo], axis=0)
    lane128 = iota((64, 128), 1)
    row128 = iota((64, 128), 0)
    group128 = jnp.where(row128 < 8, 0, jnp.where(row128 < 16, 1, jnp.where(row128 < 24, 2, 3)))
    stat = jnp.where(lane128 == group128, block_mean, 0.0) + jnp.where(lane128 == 4, spread, 0.0)
    stat_t = jnp.transpose(jnp.concatenate([stat, stat], axis=0))[0:16, :]

    local[0].wait()
    g_embed.wait()
    embedded = (nn(normed[:, 0:WIDTH], E2[0]) + nn(normed[:, WIDTH:ENC], E2[1])).astype(BF16)
    attn_vis = (norm(embedded.astype(F32) + vis_code) * attn_gain).astype(BF16)
    local[1].wait()
    g_qkv.wait()
    qk = nt(attn_vis[:, 0:384], W2[0, 0:384, :]) + nt(attn_vis[:, 384:768], W2[1, 0:384, :])
    kv = nt(attn_vis[:, 0:384], W2[0, LOCAL:576, :]) + nt(attn_vis[:, 384:768], W2[1, LOCAL:576, :])
    lane16 = iota((16, 384), 1)
    row16 = fiota((16, 1), 0)

    def pick(low, high, shift):
        return select(row16, jnp.where((row16 >= low) & (row16 < high), row16 + shift, -1.0), 16)

    first, second, third = pick(0, 6, 0), pick(0, 6, 6), pick(6, 12, -6)

    def pack(pair, keys_values):
        left = jnp.where(lane16 < LOCAL, pair, 0.0).astype(BF16)
        right = jnp.where(lane16 >= LOCAL, pltpu.roll(pair, LOCAL, 1), 0.0).astype(BF16)
        return nn(first, left) + nn(second, right) + nn(keys_values, kv.astype(BF16))

    vhi = jnp.floor((vids + 0.5) * (1.0 / 128.0))
    vlo = vids - 128.0 * vhi
    row_ids = iota((16, 128), 0)
    id_part = jnp.where(row_ids == 12, vhi, jnp.where(row_ids == 13, vlo, 0.0))
    id_part = jnp.concatenate([id_part, jnp.zeros((16, 256), F32)], axis=1)
    P1[...] = (pack(qk, third) + id_part).astype(BF16)
    quarter = pltpu.roll(embedded.astype(F32), (WIDTH - m * LOCAL) % WIDTH, 1)[:, 0:384]
    P2[...] = pack(quarter, pick(6, 12, 0)).astype(BF16)
    R1[z] = P1[...]
    R2[y] = P2[...]

    def p1_copy(k):
        return remote(P1, R1.at[z], p1s.at[k], p1r.at[k], zdev(k))

    def p2_copy(k):
        return remote(P2, R2.at[y], p2s.at[k], p2r.at[k], ydev(k))

    g_p1 = Group(p1_copy, 8, from_z, R1, p1r)
    g_p2 = Group(p2_copy, 8, from_y, R2, p2r)
    g_up = weight(2, up_w, U2)
    g_down = weight(3, down_w, D2)

    kv_w0, kv_w1 = W2[0, LOCAL:576, :], W2[1, LOCAL:576, :]
    proj = nt(kv_w0, pieces[:, 0:384]) + nt(kv_w1, pieces[:, 384:768])
    proj = proj + pltpu.roll(proj, 64, 1)
    proj_hi = proj.astype(BF16)
    lane_p = iota((384, 128), 1)
    kv_table = jnp.where(lane_p < 64, proj_hi.astype(F32), proj - proj_hi.astype(F32)).astype(BF16)
    stat_hi = stat_t.astype(BF16)
    stat_table = jnp.where(
        iota((16, 128), 1) < 64, stat_hi.astype(F32), stat_t - stat_hi.astype(F32)
    ).astype(BF16)
    big_table = jnp.concatenate([kv_table, stat_table], axis=0)

    stream0 = mask_row + own_code
    attn_own = (norm(stream0) * attn_gain).astype(BF16)
    q_masked = nt(attn_own[:, 0:384], W2[0, 0:256, :]) + nt(attn_own[:, 384:768], W2[1, 0:256, :])

    def build(c):
        width = 512
        start = pl.multiple_of(c * width, width)
        patch = (iota((1, width), 1) + start).astype(F32)
        c0, c1, c2, c3 = coordinates(patch)
        sub = fiota((64, width), 0)
        value = jnp.where(
            sub < 8, c0, jnp.where(sub < 16, c1 + 8, jnp.where(sub < 24, c2 + 16, c3 + 24))
        )
        hot = jnp.where(sub == value, 1.0, 0.0).astype(BF16)
        raw = nn(big_table, jnp.concatenate([hot, hot], axis=0))
        m0, m1, m2, m3 = raw[384:385], raw[385:386], raw[386:387], raw[387:388]
        mean = (m0 + m1 + m2 + m3) * 0.25
        between = (m0 - mean) ** 2 + (m1 - mean) ** 2 + (m2 - mean) ** 2 + (m3 - mean) ** 2
        scale = lax.rsqrt(raw[388:389] * (1.0 / 768.0) + between * 0.25 + 1e-06)
        KT[0:LOCAL, pl.ds(start, width)] = (raw[0:LOCAL] * scale).astype(BF16)
        VT[HD:256, pl.ds(start, width)] = (raw[LOCAL:384] * scale).astype(BF16)
        KT[LOCAL:256, pl.ds(start, width)] = jnp.zeros((64, width), BF16)
        VT[0:HD, pl.ds(start, width)] = jnp.zeros((64, width), BF16)

    lax.fori_loop(0, 6, lambda c, x: (build(c), x)[1], 0)

    g_p1.wait()
    g_p2.wait()
    col = fiota((112, 1), 0)
    small = jnp.where(col < 48, col, col - 48)
    src = jnp.floor((small + 0.5) * (1.0 / 6.0))
    src = 16.0 * src + (small - 6.0 * src) + jnp.where(col < 48, 0.0, 6.0)
    src = jnp.where(col < 96, src, jnp.where(col < 104, 16.0 * (col - 96) + 12, 16.0 * (col - 104) + 13))
    chooser = select(col, src, 128)
    got1 = nn(chooser, R1[...].reshape(128, 384))
    got2 = nn(chooser[0:96], R2[...].reshape(128, 384))
    GQ[y] = got1[0:48].astype(BF16)
    GK1[y] = got1[48:96].astype(BF16)
    IDG[y] = 128.0 * got1[96:104, 0:128] + got1[104:112, 0:128]
    GE[z] = got2[0:48].astype(BF16)
    GK2[z] = got2[48:96].astype(BF16)

    def over(n, ref, slot, source, send, recv, device):
        def copy(k):
            return remote(ref.at[slot], ref.at[slot], send.at[k], recv.at[k], device(k))

        return Group(copy, n, source, ref, recv)

    r_ids = Ring(IDG, y, ydev, 4, (ids_ps, ids_pr, ids_ms, ids_mr))
    r_q = Ring(GQ, y, ydev, 4, (q_ps, q_pr, q_ms, q_mr))
    r_e = Ring(GE, z, zdev, 4, (e_ps, e_pr, e_ms, e_mr))

    def build_some(low, high):
        lax.fori_loop(low, high, lambda c, x: (build(c), x)[1], 0)

    def hop_early(t):
        r_ids.hop(t)
        r_q.hop(t)
        r_e.hop(t)

    build_some(6, 9)
    hop_early(1)
    local[4].wait()
    local[5].wait()
    g_oa.wait()
    g_ob.wait()
    forward_a = Single(remote(OA.at[s], OA.at[s], fs.at[0], fr.at[0], partner))
    forward_b = Single(remote(OB.at[s], OB.at[s], fs.at[1], fr.at[1], partner))
    build_some(9, 12)
    hop_early(2)
    build_some(12, 15)
    hop_early(3)
    r_k1 = Ring(GK1, y, ydev, 3, (k1_ps, k1_pr, k1_ms, k1_mr))
    r_k2 = Ring(GK2, z, zdev, 3, (k2_ps, k2_pr, k2_ms, k2_mr))
    build_some(15, 17)
    hop_early(4)

    ids = IDG[...].reshape(64, 128)
    lane_i = fiota((64, 128), 1)
    source = fiota((64, 1), 0) + 1.0
    hots, where_d, where_i = [], [], []
    for i in range(VIS_DEV):
        one = ids[:, i : i + 1]
        high = jnp.floor((one + 0.5) * (1.0 / 128.0))
        low = one - 128.0 * high
        hots.append(jnp.where(lane_i == high, 1.0, 0.0))
        hot = jnp.where(lane_i == low, 1.0, 0.0)
        where_d.append((hot * source).astype(BF16))
        where_i.append((hot * float(i)).astype(BF16))
    hot_t = jnp.transpose(jnp.concatenate(hots, axis=0)).astype(BF16)
    found = nn(
        hot_t,
        jnp.concatenate(
            [jnp.concatenate(where_d, axis=0), jnp.concatenate(where_i, axis=0)], axis=1
        ),
    )
    seen = found[:, 0:128]
    patch2 = fiota((128, 128), 0) * 128.0 + fiota((128, 128), 1)
    bias = jnp.where((seen > 0.5) | (patch2 >= PATCHES), NEG, 0.0)
    sub16 = iota((16, 128), 0)
    for h in range(68):
        KT[LOCAL : LOCAL + 16, h * 128 : (h + 1) * 128] = jnp.where(
            sub16 == 0, jnp.broadcast_to(bias[h : h + 1, :], (16, 128)), 0.0
        ).astype(BF16)
    own_hi = jnp.floor((own_ids + 0.5) * (1.0 / 128.0))
    own_lo = own_ids - 128.0 * own_hi
    hit_hi = jnp.where(lane_row == own_hi, 1.0, 0.0).astype(BF16)
    hit_lo = lane_row == own_lo
    place = nn(hit_hi, found.astype(BF16))
    own_d = jnp.sum(jnp.where(hit_lo, place[:, 0:128], 0.0), axis=1, keepdims=True) - 1.0
    own_i = jnp.sum(jnp.where(hit_lo, place[:, 128:256], 0.0), axis=1, keepdims=True)
    is_vis = own_d > -0.5
    late = own_i > 5.5
    own_i6 = jnp.where(late, own_i - 6.0, own_i)
    own_y = jnp.floor((own_d + 0.5) * 0.125)
    own_z = own_d - 8.0 * own_y
    row_yz = own_y * 48.0 + own_z * 6.0 + own_i6
    row_zy = own_z * 48.0 + own_y * 6.0 + own_i6

    def choose(row, gathered):
        lane = fiota((ROWS, 384), 1)
        hit = jnp.where((lane == row) & is_vis, 1.0, 0.0)
        one = nn(jnp.where(late, 0.0, hit).astype(BF16), gathered)
        two = nn(jnp.where(late, hit, 0.0).astype(BF16), gathered)
        both = one + pltpu.roll(two, LOCAL, 1)
        return jnp.where(iota((ROWS, 256), 1) < LOCAL, both[:, 0:256], 0.0)

    q_vis = choose(row_yz, GQ[...].reshape(384, 384))
    queries = jnp.where(is_vis, q_vis, q_masked).astype(BF16).astype(F32) * (HD ** -0.5)
    lane_q = iota((ROWS, 256), 1)
    for h in range(3):
        keep = (lane_q >= h * HD) & (lane_q < (h + 1) * HD)
        QB[h * ROWS : (h + 1) * ROWS, :] = jnp.where(
            keep, queries, jnp.where(lane_q == LOCAL, 1.0, 0.0)
        ).astype(BF16)

    XE[m] = choose(row_zy, GE[...].reshape(384, 384)).astype(BF16)

    c_xe = over(4, XE, m, from_x, xes, xer, xdev)

    MX[...] = jnp.full((3 * ROWS, 128), NEG, F32)
    LS[...] = jnp.zeros((3 * ROWS, 128), F32)
    ACC[...] = jnp.zeros((3 * ROWS, 256), F32)

    def absorb(scores, width, product):
        peak_old = MX[...]
        peak = jnp.maximum(peak_old, jnp.max(scores, axis=1, keepdims=True))
        factor = jnp.exp(peak_old - peak)
        weights_ = jnp.exp(scores - peak[:, 0:1])
        total = weights_[:, 0:128]
        for t in range(1, width // 128):
            total = total + weights_[:, t * 128 : (t + 1) * 128]
        MX[...] = peak
        LS[...] = LS[...] * factor + total
        ACC[...] = ACC[...] * jnp.concatenate([factor, factor], axis=1) + product(weights_.astype(BF16))

    def masked(c, x):
        r_k1.hop(c + 1)
        r_k2.hop(c + 1)
        start = pl.multiple_of(c * CHUNK, 128)
        scores = nn(QB[...], KT[:, pl.ds(start, CHUNK)])
        absorb(scores, CHUNK, lambda w: nt(w, VT[:, pl.ds(start, CHUNK)]))
        return x

    lax.fori_loop(0, KEYS // CHUNK, masked, 0)
    r_k1.waited = r_k2.waited = True

    q_only = jnp.where(iota((3 * ROWS, 256), 1) < LOCAL, QB[...].astype(F32), 0.0).astype(BF16)

    seen_rows = jnp.concatenate([GK1[...].reshape(384, 384), GK2[...].reshape(384, 384)], axis=0)
    absorb(nt(q_only, seen_rows[:, 0:256]), 768, lambda w: nn(w, seen_rows[:, 128:384]))

    context = jnp.zeros((ROWS, 256), F32)
    for h in range(3):
        keep = (lane_q >= (h + 1) * HD) & (lane_q < (h + 2) * HD)
        part = slice(h * ROWS, (h + 1) * ROWS)
        total = jnp.sum(LS[part, :], axis=1, keepdims=True)
        context = context + jnp.where(keep, ACC[part, :] / total, 0.0)
    head0 = context[:, 0:128]
    lane80 = iota((80, 128), 1)
    XC[m, 0:ROWS, :] = context[:, 128:256].astype(BF16)
    XC[m, ROWS:224, :] = jnp.where(lane80 < HD, pltpu.roll(head0[0:80], HD, 1), head0[64:ROWS]).astype(BF16)
    c_xc = over(4, XC, m, from_x, xcs, xcr, xdev)

    c_xe.wait()
    filled = jnp.zeros((ROWS, WIDTH), F32)
    for i in range(4):
        wide = jnp.concatenate([XE[i].astype(F32), jnp.zeros((ROWS, 512), F32)], axis=1)
        filled = filled + (pltpu.roll(wide, i * LOCAL, 1) if i else wide)
    stream = jnp.where(is_vis, filled, mask_row) + own_code
    STREAM[...] = stream

    local[2].wait()
    local[3].wait()
    g_up.wait()
    g_down.wait()
    forward_a.wait()
    forward_b.wait()
    c_xc.wait()
    pairs = jnp.concatenate([XC[i, 0:ROWS, :] for i in range(4)], axis=1)
    lows, highs = [], []
    for i in (0, 2):
        one, two = XC[i, ROWS:224, :].astype(F32), XC[i + 1, ROWS:224, :].astype(F32)
        lows.append(jnp.where(lane80 < HD, one, pltpu.roll(two, HD, 1)).astype(BF16))
        highs.append(jnp.where(lane80 < HD, pltpu.roll(one, HD, 1), two).astype(BF16))
    singles = jnp.concatenate(
        [jnp.concatenate(lows, axis=1), jnp.concatenate(highs, axis=1)], axis=0
    )
    for half in range(2):
        cols = slice(half * 384, (half + 1) * 384)
        most = STREAM[:, cols] + nn(pairs, OA[half].reshape(512, 384))
        rest = nn(singles, OB[half].reshape(256, 384))
        MID[0:80, cols] = most[0:80] + rest[0:80]
        MID[80:ROWS, cols] = most[80:ROWS] + rest[96:160]

    mlp_in = (norm(MID[...]) * mlp_gain).astype(BF16)
    raised = nn(mlp_in[:, 0:384], U2[0]) + nn(mlp_in[:, 384:768], U2[1])
    hidden = (0.5 * raised * (1.0 + lax.erf(raised * np.float32(np.sqrt(0.5))))).astype(BF16)
    for half in range(2):
        PB[half] = nn(hidden, D2[half]).astype(BF16)

    def quadrant(q):
        return PB.at[q % 2, pl.ds(pl.multiple_of((q // 2) * 64, 16), 80)]

    def rs_copy(k):
        return remote(quadrant((m + k) % 4), RX.at[m], rss.at[k], rsr.at[k], xdev(k))

    c_rs = Group(rs_copy, 4, from_x, RX, rsr)
    RX[m] = PB[m % 2, pl.ds(pl.multiple_of((m // 2) * 64, 16), 80), :]
    c_rs.wait()
    YX[m] = (
        RX[0].astype(F32) + RX[1].astype(F32) + RX[2].astype(F32) + RX[3].astype(F32)
    ).astype(BF16)
    c_ag = over(4, YX, m, from_x, ags, agr, xdev)
    c_ag.wait()
    for half in range(2):
        cols = slice(half * 384, (half + 1) * 384)
        result[0:80, :, cols] = (MID[0:80, cols] + YX[half].astype(F32))[:, None, :]
        result[80:OWN, :, cols] = (MID[80:OWN, cols] + YX[2 + half].astype(F32)[16:71])[:, None, :]

    finish()


def shards(
    enc_rows, vis_index, owner_of, enc_gain, embed_weight, mask_token, attn_gain, qkv_weight,
    out_weight, mlp_gain, up_weight, down_weight,
):
    qkv_t = jnp.transpose(qkv_weight, (1, 2, 0)).reshape(576, 384)
    vm = pl.BlockSpec(memory_space=pltpu.VMEM)
    hbm = pl.BlockSpec(memory_space=pl.ANY)
    dma = pltpu.SemaphoreType.DMA
    V = pltpu.VMEM
    scratch = [
        V((2, 768, 768), BF16), V((2, 576, 384), BF16), V((2, 4, 128, 384), BF16), V((2, 4, 64, 384), BF16),
        V((2, 384, 768), BF16), V((2, 768, 384), BF16), V((72, 128), jnp.int32),
        V((16, ENC), F32), V((8, 128), F32), V((16, 384), BF16), V((16, 384), BF16),
        V((8, 16, 384), BF16), V((8, 16, 384), BF16),
        V((8, 48, 384), BF16), V((8, 48, 384), BF16), V((8, 48, 384), BF16), V((8, 48, 384), BF16),
        V((8, 8, 128), F32), V((72, 128), F32),
        V((256, KEYS), BF16), V((256, KEYS), BF16),
        V((4, 224, 128), BF16), V((4, ROWS, 256), BF16),
        V((2, ROWS, 384), BF16), V((4, 80, 384), BF16), V((4, 80, 384), BF16),
        V((8, 128), F32), V((3 * ROWS, 256), BF16), V((3 * ROWS, 256), F32),
        V((3 * ROWS, 128), F32), V((3 * ROWS, 128), F32), V((ROWS, WIDTH), F32), V((ROWS, WIDTH), F32),
        dma((6,)), dma((4,)), dma((4,)), dma((4,)), dma((4,)), dma((4,)), dma((4,)), dma((2,)), dma((2,)),
    ] + [dma((8,))] * 4 + [dma((5,))] * 20 + [dma((4,))] * 8
    decoded = pl.pallas_call(
        kernel,
        out_shape=jax.ShapeDtypeStruct((OWN, 1, WIDTH), F32),
        in_specs=[vm] * 8 + [hbm, hbm, hbm, hbm, hbm],
        out_specs=vm,
        scratch_shapes=scratch,
        compiler_params=pltpu.CompilerParams(
            collective_id=0, has_side_effects=True, vmem_limit_bytes=56 * 1024 * 1024
        ),
        cost_estimate=pl.CostEstimate(flops=6_000_000_000, bytes_accessed=5_000_000, transcendentals=4_000_000),
    )(
        enc_rows, vis_index, owner_of, enc_gain, mask_token, attn_gain, mlp_gain, jnp.asarray(code_table()),
        embed_weight, qkv_t, out_weight, up_weight, down_weight,
    )
    return jnp.transpose(decoded, (1, 0, 2))


def solution(mesh):
    in_specs = (
        P("section", "seq", None),
        P("section", "seq"),
        P(),
        P(),
        P("section", None),
        P(),
        P(),
        P("section", None, "mp"),
        P("mp", "section"),
        P(),
        P("section", "mp"),
        P("mp", "section"),
    )
    out_specs = P("section", "seq", None)
    return jax.shard_map(shards, mesh=mesh, in_specs=in_specs, out_specs=out_specs, check_vma=False)
```

```python
import functools

import jax
import jax.numpy as jnp
import numpy as np
from jax import lax
from jax.experimental import pallas as pl
from jax.experimental.pallas import tpu as pltpu
from jax.sharding import PartitionSpec as P

MESH = pl.DeviceIdType.MESH
F32 = jnp.float32
BF16 = jnp.bfloat16
GX = 6
PATCHES = 8640
OWN = 135
ROWS = 144
VIS_DEV = 12
WIDTH = 768
ENC = 1536
LOCAL = 192
HD = 64
NEG = -1e30
KEYS = 8704
CHUNK = 2176


def code_table():
    half = WIDTH // 8
    frequency = (1.0 / 10000.0 ** (np.arange(half, dtype=np.float32) / half)).astype(np.float32)
    table = np.zeros((64, WIDTH), np.float32)
    for c, (base, count) in enumerate(((0, GX), (8, GX), (16, GX), (24, 40))):
        angle = np.arange(count, dtype=np.float32)[:, None] * frequency[None, :]
        table[base : base + count, c * 192 : c * 192 + half] = np.sin(angle)
        table[base : base + count, c * 192 + half : (c + 1) * 192] = np.cos(angle)
    pieces = []
    for _ in range(3):
        piece = table.astype(BF16)
        pieces.append(piece)
        table = table - piece.astype(np.float32)
    return np.concatenate(pieces, axis=0)


def iota(shape, axis):
    return lax.broadcasted_iota(jnp.int32, shape, axis)


def fiota(shape, axis):
    return iota(shape, axis).astype(F32)


def nn(a, b):
    return lax.dot_general(a, b, (((1,), (0,)), ((), ())), preferred_element_type=F32)


def nt(a, b):
    return lax.dot_general(a, b, (((1,), (1,)), ((), ())), preferred_element_type=F32)


def coordinates(patch):
    c3 = jnp.floor((patch + 0.5) * (1.0 / 216.0))
    rest = patch - 216.0 * c3
    c2 = jnp.floor((rest + 0.5) * (1.0 / 36.0))
    rest = rest - 36.0 * c2
    c1 = jnp.floor((rest + 0.5) * (1.0 / 6.0))
    return rest - 6.0 * c1, c1, c2, c3


def one_hot_rows(patch, lanes):
    c0, c1, c2, c3 = coordinates(patch)
    lane = (iota((patch.shape[0], lanes), 1) & 63).astype(F32)
    value = jnp.where(
        lane < 8, c0, jnp.where(lane < 16, c1 + 8, jnp.where(lane < 24, c2 + 16, c3 + 24))
    )
    return jnp.where(lane == value, 1.0, 0.0).astype(BF16)


def norm(values):
    centred = values - jnp.mean(values, axis=-1, keepdims=True)
    spread = jnp.mean(centred * centred, axis=-1, keepdims=True)
    return centred * lax.rsqrt(spread + 1e-06)


def select(target, source, count):
    lane = fiota((target.shape[0], count), 1)
    return jnp.where(lane == source, 1.0, 0.0).astype(BF16)


def kernel(
    enc, vis, owner, enc_g, mask_t, attn_g, mlp_g, ct3, embed_w, qkv_w, out_w, up_w, down_w,
    result,
    E2, W2, OA, OB, U2, D2, own2, encf, vrow, P1, P2, R1, R2, GQ, GE, GK1, GK2, IDG,
    rankf, KT, VT, XC, XE, PB, RX, YX, SC, QB, ACC, MX, LS, STREAM, MID,
    loc_sem, ws, wr, os_, or_, os2, or2, fs, fr, p1s, p1r, p2s, p2r,
    ids_s, ids_r, q_s, q_r, e_s, e_r, k1_s, k1_r, k2_s, k2_r,
    xcs, xcr, xes, xer, rss, rsr, ags, agr,
):
    s = lax.axis_index("section")
    seq = lax.axis_index("seq")
    m = lax.axis_index("mp")
    y = seq // 8
    z = seq % 8
    partner = {"section": 1 - s}

    def zdev(k):
        return {"seq": y * 8 + (z + k) % 8}

    def ydev(k):
        return {"seq": ((y + k) % 8) * 8 + z}

    def xdev(k):
        return {"mp": (m + k) % 4}

    def remote(src, dst, send, recv, device):
        return pltpu.make_async_remote_copy(
            src_ref=src, dst_ref=dst, send_sem=send, recv_sem=recv, device_id=device, device_id_type=MESH
        )

    def ring(n, first=1):
        def run(f):
            lax.fori_loop(first, n, lambda k, c: (f(k), c)[1], 0)

        return run

    groups = []

    class Group:
        def __init__(self, copy, n, slot, ref, recv):
            self.copy, self.n, self.slot, self.ref, self.sem = copy, n, slot, ref, recv
            self.waited = self.gone = False
            groups.append(self)
            ring(n)(lambda k: copy(k).start())

        def wait_one(self, k):
            there = self.ref.at[self.slot(k)]
            remote(there, there, self.sem.at[k], self.sem.at[k], partner).wait_recv()

        def wait(self):
            self.waited = True
            ring(self.n)(self.wait_one)

        def left(self):
            if not self.gone:
                self.gone = True
                ring(self.n)(lambda k: self.copy(k).wait_send())

    class Single:
        def __init__(self, copy):
            self.copy = copy
            self.waited = False
            groups.append(self)
            copy.start()

        def wait(self):
            self.waited = True
            self.copy.wait_recv()

        def left(self):
            self.copy.wait_send()

    class Local:
        def __init__(self, copy):
            self.copy = copy
            self.waited = False
            groups.append(self)
            copy.start()

        def wait(self):
            self.waited = True
            self.copy.wait()

        def left(self):
            pass

    def finish():
        for g in groups:
            if not g.waited:
                g.wait()
            g.left()

    def from_z(k):
        return (z + 8 - k) % 8

    def from_y(k):
        return (y + 8 - k) % 8

    def from_x(k):
        return (m + 4 - k) % 4

    def halves(ref_out, ref_in, i):
        return pltpu.make_async_copy(ref_in, ref_out.at[s], loc_sem.at[i])

    barrier = pltpu.get_barrier_semaphore()
    pl.semaphore_signal(barrier, inc=1, device_id=partner, device_id_type=MESH)
    ring(8)(lambda k: pl.semaphore_signal(barrier, inc=1, device_id=zdev(k), device_id_type=MESH))
    ring(8)(lambda k: pl.semaphore_signal(barrier, inc=1, device_id=ydev(k), device_id_type=MESH))
    ring(4)(lambda k: pl.semaphore_signal(barrier, inc=1, device_id=xdev(k), device_id_type=MESH))

    local = [
        Local(copy)
        for copy in (
            halves(E2, embed_w, 0), halves(W2, qkv_w, 1), halves(U2, up_w, 2), halves(D2, down_w, 3),
            pltpu.make_async_copy(out_w.at[pl.ds(HD, 128)], OA.at[s, m], loc_sem.at[4]),
            pltpu.make_async_copy(out_w.at[pl.ds(0, HD)], OB.at[s, m], loc_sem.at[5]),
        )
    ]

    mask_row = mask_t[...].astype(F32).reshape(1, WIDTH)
    attn_gain = attn_g[...].astype(F32).reshape(1, WIDTH)
    mlp_gain = mlp_g[...].astype(F32).reshape(1, WIDTH)
    enc_gain = jnp.concatenate(
        [enc_g[0:WIDTH].astype(F32).reshape(1, WIDTH), enc_g[WIDTH:ENC].astype(F32).reshape(1, WIDTH)], axis=1
    )
    table = ct3[...]
    vrow[...] = jnp.full((8, 128), -1.0, F32)
    vrow[0:1, 0:VIS_DEV] = vis[...].astype(F32)
    vids = vrow[0:1, :]
    vcol = jnp.sum(
        jnp.where(iota((16, 128), 1) == iota((16, 128), 0), jnp.broadcast_to(vids, (16, 128)), 0.0),
        axis=1, keepdims=True,
    )
    vis_code = nn(one_hot_rows(jnp.maximum(vcol, 0.0), 192), table)
    encf[...] = jnp.zeros((16, ENC), F32)
    encf[0:VIS_DEV, :] = enc[0].astype(F32)
    normed = (norm(encf[...]) * enc_gain).astype(BF16)

    own2[...] = jnp.full((72, 128), -1, jnp.int32)
    for i in range(8):
        own2[i * 8 : (i + 1) * 8, :] = owner[i * 1024 : (i + 1) * 1024].reshape(8, 128)
    for i in range(64, 67):
        own2[i : i + 1, :] = owner[i * 128 : (i + 1) * 128].reshape(1, 128)
    own2[67:68, 0:64] = owner[67 * 128 : PATCHES].reshape(1, 64)
    flags = jnp.where(own2[...] == seq, 1.0, 0.0).astype(F32)
    flagb = flags.astype(BF16)
    upper = jnp.where(iota((128, 128), 0) <= iota((128, 128), 1), 1.0, 0.0).astype(BF16)
    lower = jnp.where(iota((72, 72), 1) < iota((72, 72), 0), 1.0, 0.0).astype(BF16)
    within = nn(flagb, upper)
    before = jnp.sum(nn(lower, flagb), axis=1, keepdims=True)
    rankf[...] = jnp.where(flags > 0.5, within + before - 1.0, -1.0)
    own_j = fiota((ROWS, 128), 0)
    lane_row = fiota((ROWS, 128), 1)

    def find(h, total):
        row = jnp.broadcast_to(rankf[pl.ds(h, 1), :], (ROWS, 128))
        return total + jnp.where(row == own_j, lane_row + (h * 128).astype(F32), 0.0)

    own_ids = jnp.sum(
        lax.fori_loop(0, 68, find, jnp.zeros((ROWS, 128), F32), unroll=4), axis=1, keepdims=True
    )
    pl.semaphore_wait(barrier, 18)

    def weight(i, src, dst):
        return Single(remote(src, dst.at[s], ws.at[i], wr.at[i], partner))

    g_embed = weight(0, embed_w, E2)
    g_qkv = weight(1, qkv_w, W2)

    def oa_copy(k):
        return remote(out_w.at[pl.ds(HD, 128)], OA.at[s, m], os_.at[k], or_.at[k], xdev(k))

    def ob_copy(k):
        return remote(out_w.at[pl.ds(0, HD)], OB.at[s, m], os2.at[k], or2.at[k], xdev(k))

    g_oa = Group(oa_copy, 4, lambda k: (s, from_x(k)), OA, or_)
    g_ob = Group(ob_copy, 4, lambda k: (s, from_x(k)), OB, or2)
    own_code = nn(one_hot_rows(own_ids, 192), table)

    row64 = iota((64, WIDTH), 0)
    lane64 = iota((64, WIDTH), 1)
    group = jnp.where(row64 < 8, 0, jnp.where(row64 < 16, 1, jnp.where(row64 < 24, 2, 3)))
    inside = (lane64 >= group * 192) & (lane64 < group * 192 + 192)
    mask_centred = mask_row - jnp.mean(mask_row, axis=-1, keepdims=True)
    code = table[0:64].astype(F32) + table[64:128].astype(F32) + table[128:192].astype(F32)
    block = jnp.where(inside, mask_centred + code, 0.0)
    block_sum = jnp.sum(block, axis=1, keepdims=True)
    block_mean = block_sum * (1.0 / 192.0)
    off = jnp.where(inside, block - block_mean, 0.0)
    spread = jnp.sum(off * off, axis=1, keepdims=True)
    scaled = (block - block_sum * (1.0 / 768.0)) * attn_gain
    scaled_hi = scaled.astype(BF16)
    scaled_lo = (scaled - scaled_hi.astype(F32)).astype(BF16)
    pieces = jnp.concatenate([scaled_hi, scaled_lo], axis=0)
    lane128 = iota((64, 128), 1)
    row128 = iota((64, 128), 0)
    group128 = jnp.where(row128 < 8, 0, jnp.where(row128 < 16, 1, jnp.where(row128 < 24, 2, 3)))
    stat = jnp.where(lane128 == group128, block_mean, 0.0) + jnp.where(lane128 == 4, spread, 0.0)
    stat_t = jnp.transpose(jnp.concatenate([stat, stat], axis=0))[0:16, :]

    local[0].wait()
    g_embed.wait()
    embedded = (nn(normed[:, 0:WIDTH], E2[0]) + nn(normed[:, WIDTH:ENC], E2[1])).astype(BF16)
    attn_vis = (norm(embedded.astype(F32) + vis_code) * attn_gain).astype(BF16)
    local[1].wait()
    g_qkv.wait()
    qk = nt(attn_vis[:, 0:384], W2[0, 0:384, :]) + nt(attn_vis[:, 384:768], W2[1, 0:384, :])
    kv = nt(attn_vis[:, 0:384], W2[0, LOCAL:576, :]) + nt(attn_vis[:, 384:768], W2[1, LOCAL:576, :])
    lane16 = iota((16, 384), 1)
    row16 = fiota((16, 1), 0)

    def pick(low, high, shift):
        return select(row16, jnp.where((row16 >= low) & (row16 < high), row16 + shift, -1.0), 16)

    first, second, third = pick(0, 6, 0), pick(0, 6, 6), pick(6, 12, -6)

    def pack(pair, keys_values):
        left = jnp.where(lane16 < LOCAL, pair, 0.0).astype(BF16)
        right = jnp.where(lane16 >= LOCAL, pltpu.roll(pair, LOCAL, 1), 0.0).astype(BF16)
        return nn(first, left) + nn(second, right) + nn(keys_values, kv.astype(BF16))

    vhi = jnp.floor((vids + 0.5) * (1.0 / 128.0))
    vlo = vids - 128.0 * vhi
    row_ids = iota((16, 128), 0)
    id_part = jnp.where(row_ids == 12, vhi, jnp.where(row_ids == 13, vlo, 0.0))
    id_part = jnp.concatenate([id_part, jnp.zeros((16, 256), F32)], axis=1)
    P1[...] = (pack(qk, third) + id_part).astype(BF16)
    quarter = pltpu.roll(embedded.astype(F32), (WIDTH - m * LOCAL) % WIDTH, 1)[:, 0:384]
    P2[...] = pack(quarter, pick(6, 12, 0)).astype(BF16)
    R1[z] = P1[...]
    R2[y] = P2[...]

    def p1_copy(k):
        return remote(P1, R1.at[z], p1s.at[k], p1r.at[k], zdev(k))

    def p2_copy(k):
        return remote(P2, R2.at[y], p2s.at[k], p2r.at[k], ydev(k))

    g_p1 = Group(p1_copy, 8, from_z, R1, p1r)
    g_p2 = Group(p2_copy, 8, from_y, R2, p2r)
    g_up = weight(2, up_w, U2)
    g_down = weight(3, down_w, D2)

    kv_w0, kv_w1 = W2[0, LOCAL:576, :], W2[1, LOCAL:576, :]
    proj = nt(kv_w0, pieces[:, 0:384]) + nt(kv_w1, pieces[:, 384:768])
    proj = proj + pltpu.roll(proj, 64, 1)
    proj_hi = proj.astype(BF16)
    lane_p = iota((384, 128), 1)
    kv_table = jnp.where(lane_p < 64, proj_hi.astype(F32), proj - proj_hi.astype(F32)).astype(BF16)
    stat_hi = stat_t.astype(BF16)
    stat_table = jnp.where(
        iota((16, 128), 1) < 64, stat_hi.astype(F32), stat_t - stat_hi.astype(F32)
    ).astype(BF16)
    big_table = jnp.concatenate([kv_table, stat_table], axis=0)

    stream0 = mask_row + own_code
    attn_own = (norm(stream0) * attn_gain).astype(BF16)
    q_masked = nt(attn_own[:, 0:384], W2[0, 0:256, :]) + nt(attn_own[:, 384:768], W2[1, 0:256, :])

    def build(c):
        width = 512
        start = pl.multiple_of(c * width, width)
        patch = (iota((1, width), 1) + start).astype(F32)
        c0, c1, c2, c3 = coordinates(patch)
        sub = fiota((64, width), 0)
        value = jnp.where(
            sub < 8, c0, jnp.where(sub < 16, c1 + 8, jnp.where(sub < 24, c2 + 16, c3 + 24))
        )
        hot = jnp.where(sub == value, 1.0, 0.0).astype(BF16)
        raw = nn(big_table, jnp.concatenate([hot, hot], axis=0))
        m0, m1, m2, m3 = raw[384:385], raw[385:386], raw[386:387], raw[387:388]
        mean = (m0 + m1 + m2 + m3) * 0.25
        between = (m0 - mean) ** 2 + (m1 - mean) ** 2 + (m2 - mean) ** 2 + (m3 - mean) ** 2
        scale = lax.rsqrt(raw[388:389] * (1.0 / 768.0) + between * 0.25 + 1e-06)
        KT[0:LOCAL, pl.ds(start, width)] = (raw[0:LOCAL] * scale).astype(BF16)
        VT[HD:256, pl.ds(start, width)] = (raw[LOCAL:384] * scale).astype(BF16)
        KT[LOCAL:256, pl.ds(start, width)] = jnp.zeros((64, width), BF16)
        VT[0:HD, pl.ds(start, width)] = jnp.zeros((64, width), BF16)

    lax.fori_loop(0, 6, lambda c, x: (build(c), x)[1], 0)

    g_p1.wait()
    g_p2.wait()
    col = fiota((112, 1), 0)
    small = jnp.where(col < 48, col, col - 48)
    src = jnp.floor((small + 0.5) * (1.0 / 6.0))
    src = 16.0 * src + (small - 6.0 * src) + jnp.where(col < 48, 0.0, 6.0)
    src = jnp.where(col < 96, src, jnp.where(col < 104, 16.0 * (col - 96) + 12, 16.0 * (col - 104) + 13))
    chooser = select(col, src, 128)
    got1 = nn(chooser, R1[...].reshape(128, 384))
    got2 = nn(chooser[0:96], R2[...].reshape(128, 384))
    GQ[y] = got1[0:48].astype(BF16)
    GK1[y] = got1[48:96].astype(BF16)
    IDG[y] = 128.0 * got1[96:104, 0:128] + got1[104:112, 0:128]
    GE[z] = got2[0:48].astype(BF16)
    GK2[z] = got2[48:96].astype(BF16)

    def over(n, ref, slot, source, send, recv, device):
        def copy(k):
            return remote(ref.at[slot], ref.at[slot], send.at[k], recv.at[k], device(k))

        return Group(copy, n, source, ref, recv)

    c_q = over(8, GQ, y, from_y, q_s, q_r, ydev)
    c_ids = over(8, IDG, y, from_y, ids_s, ids_r, ydev)
    c_e = over(8, GE, z, from_z, e_s, e_r, zdev)

    def build_some(low, high):
        lax.fori_loop(low, high, lambda c, x: (build(c), x)[1], 0)

    local[4].wait()
    local[5].wait()
    g_oa.wait()
    g_ob.wait()
    forward_a = Single(remote(OA.at[s], OA.at[s], fs.at[0], fr.at[0], partner))
    forward_b = Single(remote(OB.at[s], OB.at[s], fs.at[1], fr.at[1], partner))
    build_some(6, 13)
    c_q.left()
    c_k1 = over(8, GK1, y, from_y, k1_s, k1_r, ydev)
    c_e.left()
    c_k2 = over(8, GK2, z, from_z, k2_s, k2_r, zdev)
    build_some(13, 17)
    c_ids.wait()

    ids = IDG[...].reshape(64, 128)
    lane_i = fiota((64, 128), 1)
    source = fiota((64, 1), 0) + 1.0
    hots, where_d, where_i = [], [], []
    for i in range(VIS_DEV):
        one = ids[:, i : i + 1]
        high = jnp.floor((one + 0.5) * (1.0 / 128.0))
        low = one - 128.0 * high
        hots.append(jnp.where(lane_i == high, 1.0, 0.0))
        hot = jnp.where(lane_i == low, 1.0, 0.0)
        where_d.append((hot * source).astype(BF16))
        where_i.append((hot * float(i)).astype(BF16))
    hot_t = jnp.transpose(jnp.concatenate(hots, axis=0)).astype(BF16)
    found = nn(
        hot_t,
        jnp.concatenate(
            [jnp.concatenate(where_d, axis=0), jnp.concatenate(where_i, axis=0)], axis=1
        ),
    )
    seen = found[:, 0:128]
    patch2 = fiota((128, 128), 0) * 128.0 + fiota((128, 128), 1)
    bias = jnp.where((seen > 0.5) | (patch2 >= PATCHES), NEG, 0.0)
    sub16 = iota((16, 128), 0)
    for h in range(68):
        KT[LOCAL : LOCAL + 16, h * 128 : (h + 1) * 128] = jnp.where(
            sub16 == 0, jnp.broadcast_to(bias[h : h + 1, :], (16, 128)), 0.0
        ).astype(BF16)
    own_hi = jnp.floor((own_ids + 0.5) * (1.0 / 128.0))
    own_lo = own_ids - 128.0 * own_hi
    hit_hi = jnp.where(lane_row == own_hi, 1.0, 0.0).astype(BF16)
    hit_lo = lane_row == own_lo
    place = nn(hit_hi, found.astype(BF16))
    own_d = jnp.sum(jnp.where(hit_lo, place[:, 0:128], 0.0), axis=1, keepdims=True) - 1.0
    own_i = jnp.sum(jnp.where(hit_lo, place[:, 128:256], 0.0), axis=1, keepdims=True)
    is_vis = own_d > -0.5
    late = own_i > 5.5
    own_i6 = jnp.where(late, own_i - 6.0, own_i)
    own_y = jnp.floor((own_d + 0.5) * 0.125)
    own_z = own_d - 8.0 * own_y
    row_yz = own_y * 48.0 + own_z * 6.0 + own_i6
    row_zy = own_z * 48.0 + own_y * 6.0 + own_i6

    def choose(row, gathered):
        lane = fiota((ROWS, 384), 1)
        hit = jnp.where((lane == row) & is_vis, 1.0, 0.0)
        one = nn(jnp.where(late, 0.0, hit).astype(BF16), gathered)
        two = nn(jnp.where(late, hit, 0.0).astype(BF16), gathered)
        both = one + pltpu.roll(two, LOCAL, 1)
        return jnp.where(iota((ROWS, 256), 1) < LOCAL, both[:, 0:256], 0.0)

    c_q.wait()
    q_vis = choose(row_yz, GQ[...].reshape(384, 384))
    queries = jnp.where(is_vis, q_vis, q_masked).astype(BF16).astype(F32) * (HD ** -0.5)
    lane_q = iota((ROWS, 256), 1)
    for h in range(3):
        keep = (lane_q >= h * HD) & (lane_q < (h + 1) * HD)
        QB[h * ROWS : (h + 1) * ROWS, :] = jnp.where(
            keep, queries, jnp.where(lane_q == LOCAL, 1.0, 0.0)
        ).astype(BF16)

    c_e.wait()
    XE[m] = choose(row_zy, GE[...].reshape(384, 384)).astype(BF16)

    c_xe = over(4, XE, m, from_x, xes, xer, xdev)

    MX[...] = jnp.full((3 * ROWS, 128), NEG, F32)
    LS[...] = jnp.zeros((3 * ROWS, 128), F32)
    ACC[...] = jnp.zeros((3 * ROWS, 256), F32)

    def absorb(scores, width, product):
        peak_old = MX[...]
        peak = jnp.maximum(peak_old, jnp.max(scores, axis=1, keepdims=True))
        factor = jnp.exp(peak_old - peak)
        weights_ = jnp.exp(scores - peak[:, 0:1])
        total = weights_[:, 0:128]
        for t in range(1, width // 128):
            total = total + weights_[:, t * 128 : (t + 1) * 128]
        MX[...] = peak
        LS[...] = LS[...] * factor + total
        ACC[...] = ACC[...] * jnp.concatenate([factor, factor], axis=1) + product(weights_.astype(BF16))

    def masked(c, x):
        start = pl.multiple_of(c * CHUNK, 128)
        scores = nn(QB[...], KT[:, pl.ds(start, CHUNK)])
        absorb(scores, CHUNK, lambda w: nt(w, VT[:, pl.ds(start, CHUNK)]))
        return x

    lax.fori_loop(0, KEYS // CHUNK, masked, 0)

    c_k1.wait()
    c_k2.wait()
    q_only = jnp.where(iota((3 * ROWS, 256), 1) < LOCAL, QB[...].astype(F32), 0.0).astype(BF16)

    seen_rows = jnp.concatenate([GK1[...].reshape(384, 384), GK2[...].reshape(384, 384)], axis=0)
    absorb(nt(q_only, seen_rows[:, 0:256]), 768, lambda w: nn(w, seen_rows[:, 128:384]))

    context = jnp.zeros((ROWS, 256), F32)
    for h in range(3):
        keep = (lane_q >= (h + 1) * HD) & (lane_q < (h + 2) * HD)
        part = slice(h * ROWS, (h + 1) * ROWS)
        total = jnp.sum(LS[part, :], axis=1, keepdims=True)
        context = context + jnp.where(keep, ACC[part, :] / total, 0.0)
    head0 = context[:, 0:128]
    lane80 = iota((80, 128), 1)
    XC[m, 0:ROWS, :] = context[:, 128:256].astype(BF16)
    XC[m, ROWS:224, :] = jnp.where(lane80 < HD, pltpu.roll(head0[0:80], HD, 1), head0[64:ROWS]).astype(BF16)
    c_xc = over(4, XC, m, from_x, xcs, xcr, xdev)

    c_xe.wait()
    filled = jnp.zeros((ROWS, WIDTH), F32)
    for i in range(4):
        wide = jnp.concatenate([XE[i].astype(F32), jnp.zeros((ROWS, 512), F32)], axis=1)
        filled = filled + (pltpu.roll(wide, i * LOCAL, 1) if i else wide)
    stream = jnp.where(is_vis, filled, mask_row) + own_code
    STREAM[...] = stream

    local[2].wait()
    local[3].wait()
    g_up.wait()
    g_down.wait()
    forward_a.wait()
    forward_b.wait()
    c_xc.wait()
    pairs = jnp.concatenate([XC[i, 0:ROWS, :] for i in range(4)], axis=1)
    lows, highs = [], []
    for i in (0, 2):
        one, two = XC[i, ROWS:224, :].astype(F32), XC[i + 1, ROWS:224, :].astype(F32)
        lows.append(jnp.where(lane80 < HD, one, pltpu.roll(two, HD, 1)).astype(BF16))
        highs.append(jnp.where(lane80 < HD, pltpu.roll(one, HD, 1), two).astype(BF16))
    singles = jnp.concatenate(
        [jnp.concatenate(lows, axis=1), jnp.concatenate(highs, axis=1)], axis=0
    )
    for half in range(2):
        cols = slice(half * 384, (half + 1) * 384)
        most = STREAM[:, cols] + nn(pairs, OA[half].reshape(512, 384))
        rest = nn(singles, OB[half].reshape(256, 384))
        MID[0:80, cols] = most[0:80] + rest[0:80]
        MID[80:ROWS, cols] = most[80:ROWS] + rest[96:160]

    mlp_in = (norm(MID[...]) * mlp_gain).astype(BF16)
    raised = nn(mlp_in[:, 0:384], U2[0]) + nn(mlp_in[:, 384:768], U2[1])
    hidden = (0.5 * raised * (1.0 + lax.erf(raised * np.float32(np.sqrt(0.5))))).astype(BF16)
    for half in range(2):
        PB[half] = nn(hidden, D2[half]).astype(BF16)

    def quadrant(q):
        return PB.at[q % 2, pl.ds(pl.multiple_of((q // 2) * 64, 16), 80)]

    def rs_copy(k):
        return remote(quadrant((m + k) % 4), RX.at[m], rss.at[k], rsr.at[k], xdev(k))

    c_rs = Group(rs_copy, 4, from_x, RX, rsr)
    RX[m] = PB[m % 2, pl.ds(pl.multiple_of((m // 2) * 64, 16), 80), :]
    c_rs.wait()
    YX[m] = (
        RX[0].astype(F32) + RX[1].astype(F32) + RX[2].astype(F32) + RX[3].astype(F32)
    ).astype(BF16)
    c_ag = over(4, YX, m, from_x, ags, agr, xdev)
    c_ag.wait()
    for half in range(2):
        cols = slice(half * 384, (half + 1) * 384)
        result[0:80, :, cols] = (MID[0:80, cols] + YX[half].astype(F32))[:, None, :]
        result[80:OWN, :, cols] = (MID[80:OWN, cols] + YX[2 + half].astype(F32)[16:71])[:, None, :]

    finish()


def shards(
    enc_rows, vis_index, owner_of, enc_gain, embed_weight, mask_token, attn_gain, qkv_weight,
    out_weight, mlp_gain, up_weight, down_weight,
):
    qkv_t = jnp.transpose(qkv_weight, (1, 2, 0)).reshape(576, 384)
    vm = pl.BlockSpec(memory_space=pltpu.VMEM)
    hbm = pl.BlockSpec(memory_space=pl.ANY)
    dma = pltpu.SemaphoreType.DMA
    V = pltpu.VMEM
    scratch = [
        V((2, 768, 768), BF16), V((2, 576, 384), BF16), V((2, 4, 128, 384), BF16), V((2, 4, 64, 384), BF16),
        V((2, 384, 768), BF16), V((2, 768, 384), BF16), V((72, 128), jnp.int32),
        V((16, ENC), F32), V((8, 128), F32), V((16, 384), BF16), V((16, 384), BF16),
        V((8, 16, 384), BF16), V((8, 16, 384), BF16),
        V((8, 48, 384), BF16), V((8, 48, 384), BF16), V((8, 48, 384), BF16), V((8, 48, 384), BF16),
        V((8, 8, 128), F32), V((72, 128), F32),
        V((256, KEYS), BF16), V((256, KEYS), BF16),
        V((4, 224, 128), BF16), V((4, ROWS, 256), BF16),
        V((2, ROWS, 384), BF16), V((4, 80, 384), BF16), V((4, 80, 384), BF16),
        V((8, 128), F32), V((3 * ROWS, 256), BF16), V((3 * ROWS, 256), F32),
        V((3 * ROWS, 128), F32), V((3 * ROWS, 128), F32), V((ROWS, WIDTH), F32), V((ROWS, WIDTH), F32),
        dma((6,)), dma((4,)), dma((4,)), dma((4,)), dma((4,)), dma((4,)), dma((4,)), dma((2,)), dma((2,)),
    ] + [dma((8,))] * 14 + [dma((4,))] * 8
    decoded = pl.pallas_call(
        kernel,
        out_shape=jax.ShapeDtypeStruct((OWN, 1, WIDTH), F32),
        in_specs=[vm] * 8 + [hbm, hbm, hbm, hbm, hbm],
        out_specs=vm,
        scratch_shapes=scratch,
        compiler_params=pltpu.CompilerParams(
            collective_id=0, has_side_effects=True, vmem_limit_bytes=56 * 1024 * 1024
        ),
        cost_estimate=pl.CostEstimate(flops=6_000_000_000, bytes_accessed=5_000_000, transcendentals=4_000_000),
    )(
        enc_rows, vis_index, owner_of, enc_gain, mask_token, attn_gain, mlp_gain, jnp.asarray(code_table()),
        embed_weight, qkv_t, out_weight, up_weight, down_weight,
    )
    return jnp.transpose(decoded, (1, 0, 2))


def solution(mesh):
    in_specs = (
        P("section", "seq", None),
        P("section", "seq"),
        P(),
        P(),
        P("section", None),
        P(),
        P(),
        P("section", None, "mp"),
        P("mp", "section"),
        P(),
        P("section", "mp"),
        P("mp", "section"),
    )
    out_specs = P("section", "seq", None)
    return jax.shard_map(shards, mesh=mesh, in_specs=in_specs, out_specs=out_specs, check_vma=False)
```

```python
import functools

import jax
import jax.numpy as jnp
import numpy as np
from jax import lax
from jax.experimental import pallas as pl
from jax.experimental.pallas import tpu as pltpu
from jax.sharding import PartitionSpec as P

MESH = pl.DeviceIdType.MESH
F32 = jnp.float32
BF16 = jnp.bfloat16
GX = 6
PATCHES = 8640
OWN = 135
ROWS = 144
VIS_DEV = 12
WIDTH = 768
ENC = 1536
LOCAL = 192
HD = 64
NEG = -1e30
KEYS = 8704
CHUNK = 2176


def code_table():
    half = WIDTH // 8
    frequency = (1.0 / 10000.0 ** (np.arange(half, dtype=np.float32) / half)).astype(np.float32)
    table = np.zeros((64, WIDTH), np.float32)
    for c, (base, count) in enumerate(((0, GX), (8, GX), (16, GX), (24, 40))):
        angle = np.arange(count, dtype=np.float32)[:, None] * frequency[None, :]
        table[base : base + count, c * 192 : c * 192 + half] = np.sin(angle)
        table[base : base + count, c * 192 + half : (c + 1) * 192] = np.cos(angle)
    pieces = []
    for _ in range(3):
        piece = table.astype(BF16)
        pieces.append(piece)
        table = table - piece.astype(np.float32)
    return np.concatenate(pieces, axis=0)


def iota(shape, axis):
    return lax.broadcasted_iota(jnp.int32, shape, axis)


def fiota(shape, axis):
    return iota(shape, axis).astype(F32)


def nn(a, b):
    return lax.dot_general(a, b, (((1,), (0,)), ((), ())), preferred_element_type=F32)


def nt(a, b):
    return lax.dot_general(a, b, (((1,), (1,)), ((), ())), preferred_element_type=F32)


def coordinates(patch):
    c3 = jnp.floor((patch + 0.5) * (1.0 / 216.0))
    rest = patch - 216.0 * c3
    c2 = jnp.floor((rest + 0.5) * (1.0 / 36.0))
    rest = rest - 36.0 * c2
    c1 = jnp.floor((rest + 0.5) * (1.0 / 6.0))
    return rest - 6.0 * c1, c1, c2, c3


def one_hot_rows(patch, lanes):
    c0, c1, c2, c3 = coordinates(patch)
    lane = (iota((patch.shape[0], lanes), 1) & 63).astype(F32)
    value = jnp.where(
        lane < 8, c0, jnp.where(lane < 16, c1 + 8, jnp.where(lane < 24, c2 + 16, c3 + 24))
    )
    return jnp.where(lane == value, 1.0, 0.0).astype(BF16)


def norm(values):
    centred = values - jnp.mean(values, axis=-1, keepdims=True)
    spread = jnp.mean(centred * centred, axis=-1, keepdims=True)
    return centred * lax.rsqrt(spread + 1e-06)


def select(target, source, count):
    lane = fiota((target.shape[0], count), 1)
    return jnp.where(lane == source, 1.0, 0.0).astype(BF16)


def kernel(
    enc, vis, owner, enc_g, mask_t, attn_g, mlp_g, ct3, embed_w, qkv_w, out_w, up_w, down_w,
    result,
    E2, W2, OA, OB, U2, D2, own2, encf, vrow, P1, P2, R1, R2, GQ, GE, GK1, GK2, IDG,
    rankf, KT, VT, XC, XE, PB, RX, YX, SC, QB, ACC, MX, LS, STREAM, MID,
    loc_sem, ws, wr, os_, or_, os2, or2, fs, fr, p1s, p1r, p2s, p2r,
    ids_s, ids_r, q_s, q_r, e_s, e_r, k1_s, k1_r, k2_s, k2_r,
    xcs, xcr, xes, xer, rss, rsr, ags, agr,
):
    s = lax.axis_index("section")
    seq = lax.axis_index("seq")
    m = lax.axis_index("mp")
    y = seq // 8
    z = seq % 8
    partner = {"section": 1 - s}

    def zdev(k):
        return {"seq": y * 8 + (z + k) % 8}

    def ydev(k):
        return {"seq": ((y + k) % 8) * 8 + z}

    def xdev(k):
        return {"mp": (m + k) % 4}

    def remote(src, dst, send, recv, device):
        return pltpu.make_async_remote_copy(
            src_ref=src, dst_ref=dst, send_sem=send, recv_sem=recv, device_id=device, device_id_type=MESH
        )

    def ring(n):
        def run(f):
            lax.fori_loop(1, n, lambda k, c: (f(k), c)[1], 0)

        return run

    def far_first(n):
        def run(f):
            lax.fori_loop(
                0, n - 1, lambda j, c: (f(n // 2 + ((j + 1) // 2) * (1 - 2 * (j % 2))), c)[1], 0
            )

        return run

    groups = []

    class Group:
        def __init__(self, copy, n, slot, ref, recv):
            self.copy, self.n, self.slot, self.ref, self.sem = copy, n, slot, ref, recv
            self.waited = self.gone = False
            groups.append(self)
            far_first(n)(lambda k: copy(k).start())

        def wait_one(self, k):
            there = self.ref.at[self.slot(k)]
            remote(there, there, self.sem.at[k], self.sem.at[k], partner).wait_recv()

        def wait(self):
            self.waited = True
            ring(self.n)(self.wait_one)

        def left(self):
            if not self.gone:
                self.gone = True
                ring(self.n)(lambda k: self.copy(k).wait_send())

    class Single:
        def __init__(self, copy):
            self.copy = copy
            self.waited = False
            groups.append(self)
            copy.start()

        def wait(self):
            self.waited = True
            self.copy.wait_recv()

        def left(self):
            self.copy.wait_send()

    class Local:
        def __init__(self, copy):
            self.copy = copy
            self.waited = False
            groups.append(self)
            copy.start()

        def wait(self):
            self.waited = True
            self.copy.wait()

        def left(self):
            pass

    def finish():
        for g in groups:
            if not g.waited:
                g.wait()
            g.left()

    def from_z(k):
        return (z + 8 - k) % 8

    def from_y(k):
        return (y + 8 - k) % 8

    def from_x(k):
        return (m + 4 - k) % 4

    def halves(ref_out, ref_in, i):
        return pltpu.make_async_copy(ref_in, ref_out.at[s], loc_sem.at[i])

    barrier = pltpu.get_barrier_semaphore()
    def greet(device):
        pl.semaphore_signal(barrier, inc=1, device_id=device, device_id_type=MESH)

    far_first(8)(lambda k: (greet(zdev(k)), greet(ydev(k))))
    far_first(4)(lambda k: greet(xdev(k)))
    greet(partner)

    local = [
        Local(copy)
        for copy in (
            halves(E2, embed_w, 0), halves(W2, qkv_w, 1), halves(U2, up_w, 2), halves(D2, down_w, 3),
            pltpu.make_async_copy(out_w.at[pl.ds(HD, 128)], OA.at[s, m], loc_sem.at[4]),
            pltpu.make_async_copy(out_w.at[pl.ds(0, HD)], OB.at[s, m], loc_sem.at[5]),
        )
    ]

    mask_row = mask_t[...].astype(F32).reshape(1, WIDTH)
    attn_gain = attn_g[...].astype(F32).reshape(1, WIDTH)
    mlp_gain = mlp_g[...].astype(F32).reshape(1, WIDTH)
    enc_gain = jnp.concatenate(
        [enc_g[0:WIDTH].astype(F32).reshape(1, WIDTH), enc_g[WIDTH:ENC].astype(F32).reshape(1, WIDTH)], axis=1
    )
    table = ct3[...]
    vrow[...] = jnp.full((8, 128), -1.0, F32)
    vrow[0:1, 0:VIS_DEV] = vis[...].astype(F32)
    vids = vrow[0:1, :]
    vcol = jnp.sum(
        jnp.where(iota((16, 128), 1) == iota((16, 128), 0), jnp.broadcast_to(vids, (16, 128)), 0.0),
        axis=1, keepdims=True,
    )
    vis_code = nn(one_hot_rows(jnp.maximum(vcol, 0.0), 192), table)
    encf[...] = jnp.zeros((16, ENC), F32)
    encf[0:VIS_DEV, :] = enc[0].astype(F32)
    normed = (norm(encf[...]) * enc_gain).astype(BF16)

    own2[...] = jnp.full((72, 128), -1, jnp.int32)
    for i in range(8):
        own2[i * 8 : (i + 1) * 8, :] = owner[i * 1024 : (i + 1) * 1024].reshape(8, 128)
    for i in range(64, 67):
        own2[i : i + 1, :] = owner[i * 128 : (i + 1) * 128].reshape(1, 128)
    own2[67:68, 0:64] = owner[67 * 128 : PATCHES].reshape(1, 64)
    flags = jnp.where(own2[...] == seq, 1.0, 0.0).astype(F32)
    flagb = flags.astype(BF16)
    upper = jnp.where(iota((128, 128), 0) <= iota((128, 128), 1), 1.0, 0.0).astype(BF16)
    lower = jnp.where(iota((72, 72), 1) < iota((72, 72), 0), 1.0, 0.0).astype(BF16)
    within = nn(flagb, upper)
    before = jnp.sum(nn(lower, flagb), axis=1, keepdims=True)
    rankf[...] = jnp.where(flags > 0.5, within + before - 1.0, -1.0)
    own_j = fiota((ROWS, 128), 0)
    lane_row = fiota((ROWS, 128), 1)

    def find(h, total):
        row = jnp.broadcast_to(rankf[pl.ds(h, 1), :], (ROWS, 128))
        return total + jnp.where(row == own_j, lane_row + (h * 128).astype(F32), 0.0)

    own_ids = jnp.sum(
        lax.fori_loop(0, 68, find, jnp.zeros((ROWS, 128), F32), unroll=4), axis=1, keepdims=True
    )
    pl.semaphore_wait(barrier, 18)

    def weight(i, src, dst):
        return Single(remote(src, dst.at[s], ws.at[i], wr.at[i], partner))

    g_embed = weight(0, embed_w, E2)
    g_qkv = weight(1, qkv_w, W2)

    def oa_copy(k):
        return remote(out_w.at[pl.ds(HD, 128)], OA.at[s, m], os_.at[k], or_.at[k], xdev(k))

    def ob_copy(k):
        return remote(out_w.at[pl.ds(0, HD)], OB.at[s, m], os2.at[k], or2.at[k], xdev(k))

    g_oa = Group(oa_copy, 4, lambda k: (s, from_x(k)), OA, or_)
    g_ob = Group(ob_copy, 4, lambda k: (s, from_x(k)), OB, or2)
    own_code = nn(one_hot_rows(own_ids, 192), table)

    row64 = iota((64, WIDTH), 0)
    lane64 = iota((64, WIDTH), 1)
    group = jnp.where(row64 < 8, 0, jnp.where(row64 < 16, 1, jnp.where(row64 < 24, 2, 3)))
    inside = (lane64 >= group * 192) & (lane64 < group * 192 + 192)
    mask_centred = mask_row - jnp.mean(mask_row, axis=-1, keepdims=True)
    code = table[0:64].astype(F32) + table[64:128].astype(F32) + table[128:192].astype(F32)
    block = jnp.where(inside, mask_centred + code, 0.0)
    block_sum = jnp.sum(block, axis=1, keepdims=True)
    block_mean = block_sum * (1.0 / 192.0)
    off = jnp.where(inside, block - block_mean, 0.0)
    spread = jnp.sum(off * off, axis=1, keepdims=True)
    scaled = (block - block_sum * (1.0 / 768.0)) * attn_gain
    scaled_hi = scaled.astype(BF16)
    scaled_lo = (scaled - scaled_hi.astype(F32)).astype(BF16)
    pieces = jnp.concatenate([scaled_hi, scaled_lo], axis=0)
    lane128 = iota((64, 128), 1)
    row128 = iota((64, 128), 0)
    group128 = jnp.where(row128 < 8, 0, jnp.where(row128 < 16, 1, jnp.where(row128 < 24, 2, 3)))
    stat = jnp.where(lane128 == group128, block_mean, 0.0) + jnp.where(lane128 == 4, spread, 0.0)
    stat_t = jnp.transpose(jnp.concatenate([stat, stat], axis=0))[0:16, :]

    local[0].wait()
    g_embed.wait()
    embedded = (nn(normed[:, 0:WIDTH], E2[0]) + nn(normed[:, WIDTH:ENC], E2[1])).astype(BF16)
    attn_vis = (norm(embedded.astype(F32) + vis_code) * attn_gain).astype(BF16)
    local[1].wait()
    g_qkv.wait()
    qk = nt(attn_vis[:, 0:384], W2[0, 0:384, :]) + nt(attn_vis[:, 384:768], W2[1, 0:384, :])
    kv = nt(attn_vis[:, 0:384], W2[0, LOCAL:576, :]) + nt(attn_vis[:, 384:768], W2[1, LOCAL:576, :])
    lane16 = iota((16, 384), 1)
    row16 = fiota((16, 1), 0)

    def pick(low, high, shift):
        return select(row16, jnp.where((row16 >= low) & (row16 < high), row16 + shift, -1.0), 16)

    first, second, third = pick(0, 6, 0), pick(0, 6, 6), pick(6, 12, -6)

    def pack(pair, keys_values):
        left = jnp.where(lane16 < LOCAL, pair, 0.0).astype(BF16)
        right = jnp.where(lane16 >= LOCAL, pltpu.roll(pair, LOCAL, 1), 0.0).astype(BF16)
        return nn(first, left) + nn(second, right) + nn(keys_values, kv.astype(BF16))

    vhi = jnp.floor((vids + 0.5) * (1.0 / 128.0))
    vlo = vids - 128.0 * vhi
    row_ids = iota((16, 128), 0)
    id_part = jnp.where(row_ids == 12, vhi, jnp.where(row_ids == 13, vlo, 0.0))
    id_part = jnp.concatenate([id_part, jnp.zeros((16, 256), F32)], axis=1)
    P1[...] = (pack(qk, third) + id_part).astype(BF16)
    quarter = pltpu.roll(embedded.astype(F32), (WIDTH - m * LOCAL) % WIDTH, 1)[:, 0:384]
    P2[...] = pack(quarter, pick(6, 12, 0)).astype(BF16)
    R1[z] = P1[...]
    R2[y] = P2[...]

    def p1_copy(k):
        return remote(P1, R1.at[z], p1s.at[k], p1r.at[k], zdev(k))

    def p2_copy(k):
        return remote(P2, R2.at[y], p2s.at[k], p2r.at[k], ydev(k))

    g_p1 = Group(p1_copy, 8, from_z, R1, p1r)
    g_p2 = Group(p2_copy, 8, from_y, R2, p2r)
    g_up = weight(2, up_w, U2)
    g_down = weight(3, down_w, D2)

    kv_w0, kv_w1 = W2[0, LOCAL:576, :], W2[1, LOCAL:576, :]
    proj = nt(kv_w0, pieces[:, 0:384]) + nt(kv_w1, pieces[:, 384:768])
    proj = proj + pltpu.roll(proj, 64, 1)
    proj_hi = proj.astype(BF16)
    lane_p = iota((384, 128), 1)
    kv_table = jnp.where(lane_p < 64, proj_hi.astype(F32), proj - proj_hi.astype(F32)).astype(BF16)
    stat_hi = stat_t.astype(BF16)
    stat_table = jnp.where(
        iota((16, 128), 1) < 64, stat_hi.astype(F32), stat_t - stat_hi.astype(F32)
    ).astype(BF16)
    big_table = jnp.concatenate([kv_table, stat_table], axis=0)

    stream0 = mask_row + own_code
    attn_own = (norm(stream0) * attn_gain).astype(BF16)
    q_masked = nt(attn_own[:, 0:384], W2[0, 0:256, :]) + nt(attn_own[:, 384:768], W2[1, 0:256, :])

    def build(c):
        width = 512
        start = pl.multiple_of(c * width, width)
        patch = (iota((1, width), 1) + start).astype(F32)
        c0, c1, c2, c3 = coordinates(patch)
        sub = fiota((64, width), 0)
        value = jnp.where(
            sub < 8, c0, jnp.where(sub < 16, c1 + 8, jnp.where(sub < 24, c2 + 16, c3 + 24))
        )
        hot = jnp.where(sub == value, 1.0, 0.0).astype(BF16)
        raw = nn(big_table, jnp.concatenate([hot, hot], axis=0))
        m0, m1, m2, m3 = raw[384:385], raw[385:386], raw[386:387], raw[387:388]
        mean = (m0 + m1 + m2 + m3) * 0.25
        between = (m0 - mean) ** 2 + (m1 - mean) ** 2 + (m2 - mean) ** 2 + (m3 - mean) ** 2
        scale = lax.rsqrt(raw[388:389] * (1.0 / 768.0) + between * 0.25 + 1e-06)
        KT[0:LOCAL, pl.ds(start, width)] = (raw[0:LOCAL] * scale).astype(BF16)
        VT[HD:256, pl.ds(start, width)] = (raw[LOCAL:384] * scale).astype(BF16)
        KT[LOCAL:256, pl.ds(start, width)] = jnp.zeros((64, width), BF16)
        VT[0:HD, pl.ds(start, width)] = jnp.zeros((64, width), BF16)

    lax.fori_loop(0, 6, lambda c, x: (build(c), x)[1], 0)

    g_p1.wait()
    g_p2.wait()
    col = fiota((112, 1), 0)
    small = jnp.where(col < 48, col, col - 48)
    src = jnp.floor((small + 0.5) * (1.0 / 6.0))
    src = 16.0 * src + (small - 6.0 * src) + jnp.where(col < 48, 0.0, 6.0)
    src = jnp.where(col < 96, src, jnp.where(col < 104, 16.0 * (col - 96) + 12, 16.0 * (col - 104) + 13))
    chooser = select(col, src, 128)
    got1 = nn(chooser, R1[...].reshape(128, 384))
    got2 = nn(chooser[0:96], R2[...].reshape(128, 384))
    GQ[y] = got1[0:48].astype(BF16)
    GK1[y] = got1[48:96].astype(BF16)
    IDG[y] = 128.0 * got1[96:104, 0:128] + got1[104:112, 0:128]
    GE[z] = got2[0:48].astype(BF16)
    GK2[z] = got2[48:96].astype(BF16)

    def over(n, ref, slot, source, send, recv, device):
        def copy(k):
            return remote(ref.at[slot], ref.at[slot], send.at[k], recv.at[k], device(k))

        return Group(copy, n, source, ref, recv)

    c_ids = over(8, IDG, y, from_y, ids_s, ids_r, ydev)
    c_q = over(8, GQ, y, from_y, q_s, q_r, ydev)
    c_e = over(8, GE, z, from_z, e_s, e_r, zdev)

    def build_some(low, high):
        lax.fori_loop(low, high, lambda c, x: (build(c), x)[1], 0)

    local[4].wait()
    local[5].wait()
    g_oa.wait()
    g_ob.wait()
    forward_a = Single(remote(OA.at[s], OA.at[s], fs.at[0], fr.at[0], partner))
    forward_b = Single(remote(OB.at[s], OB.at[s], fs.at[1], fr.at[1], partner))
    build_some(6, 13)
    c_k1 = over(8, GK1, y, from_y, k1_s, k1_r, ydev)
    c_k2 = over(8, GK2, z, from_z, k2_s, k2_r, zdev)
    build_some(13, 17)
    c_ids.wait()

    ids = IDG[...].reshape(64, 128)
    lane_i = fiota((64, 128), 1)
    source = fiota((64, 1), 0) + 1.0
    hots, where_d, where_i = [], [], []
    for i in range(VIS_DEV):
        one = ids[:, i : i + 1]
        high = jnp.floor((one + 0.5) * (1.0 / 128.0))
        low = one - 128.0 * high
        hots.append(jnp.where(lane_i == high, 1.0, 0.0))
        hot = jnp.where(lane_i == low, 1.0, 0.0)
        where_d.append((hot * source).astype(BF16))
        where_i.append((hot * float(i)).astype(BF16))
    hot_t = jnp.transpose(jnp.concatenate(hots, axis=0)).astype(BF16)
    found = nn(
        hot_t,
        jnp.concatenate(
            [jnp.concatenate(where_d, axis=0), jnp.concatenate(where_i, axis=0)], axis=1
        ),
    )
    seen = found[:, 0:128]
    patch2 = fiota((128, 128), 0) * 128.0 + fiota((128, 128), 1)
    bias = jnp.where((seen > 0.5) | (patch2 >= PATCHES), NEG, 0.0)
    sub16 = iota((16, 128), 0)
    for h in range(68):
        KT[LOCAL : LOCAL + 16, h * 128 : (h + 1) * 128] = jnp.where(
            sub16 == 0, jnp.broadcast_to(bias[h : h + 1, :], (16, 128)), 0.0
        ).astype(BF16)
    own_hi = jnp.floor((own_ids + 0.5) * (1.0 / 128.0))
    own_lo = own_ids - 128.0 * own_hi
    hit_hi = jnp.where(lane_row == own_hi, 1.0, 0.0).astype(BF16)
    hit_lo = lane_row == own_lo
    place = nn(hit_hi, found.astype(BF16))
    own_d = jnp.sum(jnp.where(hit_lo, place[:, 0:128], 0.0), axis=1, keepdims=True) - 1.0
    own_i = jnp.sum(jnp.where(hit_lo, place[:, 128:256], 0.0), axis=1, keepdims=True)
    is_vis = own_d > -0.5
    late = own_i > 5.5
    own_i6 = jnp.where(late, own_i - 6.0, own_i)
    own_y = jnp.floor((own_d + 0.5) * 0.125)
    own_z = own_d - 8.0 * own_y
    row_yz = own_y * 48.0 + own_z * 6.0 + own_i6
    row_zy = own_z * 48.0 + own_y * 6.0 + own_i6

    def choose(row, gathered):
        lane = fiota((ROWS, 384), 1)
        hit = jnp.where((lane == row) & is_vis, 1.0, 0.0)
        one = nn(jnp.where(late, 0.0, hit).astype(BF16), gathered)
        two = nn(jnp.where(late, hit, 0.0).astype(BF16), gathered)
        both = one + pltpu.roll(two, LOCAL, 1)
        return jnp.where(iota((ROWS, 256), 1) < LOCAL, both[:, 0:256], 0.0)

    c_q.wait()
    q_vis = choose(row_yz, GQ[...].reshape(384, 384))
    queries = jnp.where(is_vis, q_vis, q_masked).astype(BF16).astype(F32) * (HD ** -0.5)
    lane_q = iota((ROWS, 256), 1)
    for h in range(3):
        keep = (lane_q >= h * HD) & (lane_q < (h + 1) * HD)
        QB[h * ROWS : (h + 1) * ROWS, :] = jnp.where(
            keep, queries, jnp.where(lane_q == LOCAL, 1.0, 0.0)
        ).astype(BF16)

    c_e.wait()
    XE[m] = choose(row_zy, GE[...].reshape(384, 384)).astype(BF16)

    c_xe = over(4, XE, m, from_x, xes, xer, xdev)

    MX[...] = jnp.full((3 * ROWS, 128), NEG, F32)
    LS[...] = jnp.zeros((3 * ROWS, 128), F32)
    ACC[...] = jnp.zeros((3 * ROWS, 256), F32)

    def absorb(scores, width, product):
        peak_old = MX[...]
        peak = jnp.maximum(peak_old, jnp.max(scores, axis=1, keepdims=True))
        factor = jnp.exp(peak_old - peak)
        weights_ = jnp.exp(scores - peak[:, 0:1])
        total = weights_[:, 0:128]
        for t in range(1, width // 128):
            total = total + weights_[:, t * 128 : (t + 1) * 128]
        MX[...] = peak
        LS[...] = LS[...] * factor + total
        ACC[...] = ACC[...] * jnp.concatenate([factor, factor], axis=1) + product(weights_.astype(BF16))

    def masked(c, x):
        start = pl.multiple_of(c * CHUNK, 128)
        scores = nn(QB[...], KT[:, pl.ds(start, CHUNK)])
        absorb(scores, CHUNK, lambda w: nt(w, VT[:, pl.ds(start, CHUNK)]))
        return x

    lax.fori_loop(0, KEYS // CHUNK, masked, 0)

    c_k1.wait()
    c_k2.wait()
    q_only = jnp.where(iota((3 * ROWS, 256), 1) < LOCAL, QB[...].astype(F32), 0.0).astype(BF16)

    seen_rows = jnp.concatenate([GK1[...].reshape(384, 384), GK2[...].reshape(384, 384)], axis=0)
    absorb(nt(q_only, seen_rows[:, 0:256]), 768, lambda w: nn(w, seen_rows[:, 128:384]))

    context = jnp.zeros((ROWS, 256), F32)
    for h in range(3):
        keep = (lane_q >= (h + 1) * HD) & (lane_q < (h + 2) * HD)
        part = slice(h * ROWS, (h + 1) * ROWS)
        total = jnp.sum(LS[part, :], axis=1, keepdims=True)
        context = context + jnp.where(keep, ACC[part, :] / total, 0.0)
    head0 = context[:, 0:128]
    lane80 = iota((80, 128), 1)
    XC[m, 0:ROWS, :] = context[:, 128:256].astype(BF16)
    XC[m, ROWS:224, :] = jnp.where(lane80 < HD, pltpu.roll(head0[0:80], HD, 1), head0[64:ROWS]).astype(BF16)
    c_xc = over(4, XC, m, from_x, xcs, xcr, xdev)

    c_xe.wait()
    filled = jnp.zeros((ROWS, WIDTH), F32)
    for i in range(4):
        wide = jnp.concatenate([XE[i].astype(F32), jnp.zeros((ROWS, 512), F32)], axis=1)
        filled = filled + (pltpu.roll(wide, i * LOCAL, 1) if i else wide)
    stream = jnp.where(is_vis, filled, mask_row) + own_code
    STREAM[...] = stream

    local[2].wait()
    local[3].wait()
    g_up.wait()
    g_down.wait()
    forward_a.wait()
    forward_b.wait()
    c_xc.wait()
    pairs = jnp.concatenate([XC[i, 0:ROWS, :] for i in range(4)], axis=1)
    lows, highs = [], []
    for i in (0, 2):
        one, two = XC[i, ROWS:224, :].astype(F32), XC[i + 1, ROWS:224, :].astype(F32)
        lows.append(jnp.where(lane80 < HD, one, pltpu.roll(two, HD, 1)).astype(BF16))
        highs.append(jnp.where(lane80 < HD, pltpu.roll(one, HD, 1), two).astype(BF16))
    singles = jnp.concatenate(
        [jnp.concatenate(lows, axis=1), jnp.concatenate(highs, axis=1)], axis=0
    )
    for half in range(2):
        cols = slice(half * 384, (half + 1) * 384)
        most = STREAM[:, cols] + nn(pairs, OA[half].reshape(512, 384))
        rest = nn(singles, OB[half].reshape(256, 384))
        MID[0:80, cols] = most[0:80] + rest[0:80]
        MID[80:ROWS, cols] = most[80:ROWS] + rest[96:160]

    mlp_in = (norm(MID[...]) * mlp_gain).astype(BF16)
    raised = nn(mlp_in[:, 0:384], U2[0]) + nn(mlp_in[:, 384:768], U2[1])
    hidden = (0.5 * raised * (1.0 + lax.erf(raised * np.float32(np.sqrt(0.5))))).astype(BF16)
    for half in range(2):
        PB[half] = nn(hidden, D2[half]).astype(BF16)

    def quadrant(q):
        return PB.at[q % 2, pl.ds(pl.multiple_of((q // 2) * 64, 16), 80)]

    def rs_copy(k):
        return remote(quadrant((m + k) % 4), RX.at[m], rss.at[k], rsr.at[k], xdev(k))

    c_rs = Group(rs_copy, 4, from_x, RX, rsr)
    RX[m] = PB[m % 2, pl.ds(pl.multiple_of((m // 2) * 64, 16), 80), :]
    c_rs.wait()
    YX[m] = (
        RX[0].astype(F32) + RX[1].astype(F32) + RX[2].astype(F32) + RX[3].astype(F32)
    ).astype(BF16)
    c_ag = over(4, YX, m, from_x, ags, agr, xdev)
    c_ag.wait()
    for half in range(2):
        cols = slice(half * 384, (half + 1) * 384)
        result[0:80, :, cols] = (MID[0:80, cols] + YX[half].astype(F32))[:, None, :]
        result[80:OWN, :, cols] = (MID[80:OWN, cols] + YX[2 + half].astype(F32)[16:71])[:, None, :]

    finish()


def shards(
    enc_rows, vis_index, owner_of, enc_gain, embed_weight, mask_token, attn_gain, qkv_weight,
    out_weight, mlp_gain, up_weight, down_weight,
):
    qkv_t = jnp.transpose(qkv_weight, (1, 2, 0)).reshape(576, 384)
    vm = pl.BlockSpec(memory_space=pltpu.VMEM)
    hbm = pl.BlockSpec(memory_space=pl.ANY)
    dma = pltpu.SemaphoreType.DMA
    V = pltpu.VMEM
    scratch = [
        V((2, 768, 768), BF16), V((2, 576, 384), BF16), V((2, 4, 128, 384), BF16), V((2, 4, 64, 384), BF16),
        V((2, 384, 768), BF16), V((2, 768, 384), BF16), V((72, 128), jnp.int32),
        V((16, ENC), F32), V((8, 128), F32), V((16, 384), BF16), V((16, 384), BF16),
        V((8, 16, 384), BF16), V((8, 16, 384), BF16),
        V((8, 48, 384), BF16), V((8, 48, 384), BF16), V((8, 48, 384), BF16), V((8, 48, 384), BF16),
        V((8, 8, 128), F32), V((72, 128), F32),
        V((256, KEYS), BF16), V((256, KEYS), BF16),
        V((4, 224, 128), BF16), V((4, ROWS, 256), BF16),
        V((2, ROWS, 384), BF16), V((4, 80, 384), BF16), V((4, 80, 384), BF16),
        V((8, 128), F32), V((3 * ROWS, 256), BF16), V((3 * ROWS, 256), F32),
        V((3 * ROWS, 128), F32), V((3 * ROWS, 128), F32), V((ROWS, WIDTH), F32), V((ROWS, WIDTH), F32),
        dma((6,)), dma((4,)), dma((4,)), dma((4,)), dma((4,)), dma((4,)), dma((4,)), dma((2,)), dma((2,)),
    ] + [dma((8,))] * 14 + [dma((4,))] * 8
    decoded = pl.pallas_call(
        kernel,
        out_shape=jax.ShapeDtypeStruct((OWN, 1, WIDTH), F32),
        in_specs=[vm] * 8 + [hbm, hbm, hbm, hbm, hbm],
        out_specs=vm,
        scratch_shapes=scratch,
        compiler_params=pltpu.CompilerParams(
            collective_id=0, has_side_effects=True, vmem_limit_bytes=56 * 1024 * 1024
        ),
        cost_estimate=pl.CostEstimate(flops=6_000_000_000, bytes_accessed=5_000_000, transcendentals=4_000_000),
    )(
        enc_rows, vis_index, owner_of, enc_gain, mask_token, attn_gain, mlp_gain, jnp.asarray(code_table()),
        embed_weight, qkv_t, out_weight, up_weight, down_weight,
    )
    return jnp.transpose(decoded, (1, 0, 2))


def solution(mesh):
    in_specs = (
        P("section", "seq", None),
        P("section", "seq"),
        P(),
        P(),
        P("section", None),
        P(),
        P(),
        P("section", None, "mp"),
        P("mp", "section"),
        P(),
        P("section", "mp"),
        P("mp", "section"),
    )
    out_specs = P("section", "seq", None)
    return jax.shard_map(shards, mesh=mesh, in_specs=in_specs, out_specs=out_specs, check_vma=False)
```

```python
import functools

import jax
import jax.numpy as jnp
import numpy as np
from jax import lax
from jax.experimental import pallas as pl
from jax.experimental.pallas import tpu as pltpu
from jax.sharding import PartitionSpec as P

MESH = pl.DeviceIdType.MESH
F32 = jnp.float32
BF16 = jnp.bfloat16
GX = 6
PATCHES = 8640
OWN = 135
ROWS = 144
VIS_DEV = 12
WIDTH = 768
ENC = 1536
LOCAL = 192
HD = 64
NEG = -1e30
KEYS = 8704
CHUNK = 2176


def code_table():
    half = WIDTH // 8
    frequency = (1.0 / 10000.0 ** (np.arange(half, dtype=np.float32) / half)).astype(np.float32)
    table = np.zeros((64, WIDTH), np.float32)
    for c, (base, count) in enumerate(((0, GX), (8, GX), (16, GX), (24, 40))):
        angle = np.arange(count, dtype=np.float32)[:, None] * frequency[None, :]
        table[base : base + count, c * 192 : c * 192 + half] = np.sin(angle)
        table[base : base + count, c * 192 + half : (c + 1) * 192] = np.cos(angle)
    pieces = []
    for _ in range(3):
        piece = table.astype(BF16)
        pieces.append(piece)
        table = table - piece.astype(np.float32)
    return np.concatenate(pieces, axis=0)


def iota(shape, axis):
    return lax.broadcasted_iota(jnp.int32, shape, axis)


def fiota(shape, axis):
    return iota(shape, axis).astype(F32)


def nn(a, b):
    return lax.dot_general(a, b, (((1,), (0,)), ((), ())), preferred_element_type=F32)


def nt(a, b):
    return lax.dot_general(a, b, (((1,), (1,)), ((), ())), preferred_element_type=F32)


def coordinates(patch):
    c3 = jnp.floor((patch + 0.5) * (1.0 / 216.0))
    rest = patch - 216.0 * c3
    c2 = jnp.floor((rest + 0.5) * (1.0 / 36.0))
    rest = rest - 36.0 * c2
    c1 = jnp.floor((rest + 0.5) * (1.0 / 6.0))
    return rest - 6.0 * c1, c1, c2, c3


def one_hot_rows(patch, lanes):
    c0, c1, c2, c3 = coordinates(patch)
    lane = (iota((patch.shape[0], lanes), 1) & 63).astype(F32)
    value = jnp.where(
        lane < 8, c0, jnp.where(lane < 16, c1 + 8, jnp.where(lane < 24, c2 + 16, c3 + 24))
    )
    return jnp.where(lane == value, 1.0, 0.0).astype(BF16)


def norm(values):
    centred = values - jnp.mean(values, axis=-1, keepdims=True)
    spread = jnp.mean(centred * centred, axis=-1, keepdims=True)
    return centred * lax.rsqrt(spread + 1e-06)


def select(target, source, count):
    lane = fiota((target.shape[0], count), 1)
    return jnp.where(lane == source, 1.0, 0.0).astype(BF16)


def kernel(
    enc_h, vis, owner, enc_gh, mask_h, attn_h, mlp_h, ct3_h, embed_w, qkv_w, out_w, up_w, down_w,
    result,
    E2, W2, OA, OB, U2, D2, own2, enc, enc_g, mask_t, attn_g, mlp_g, ct3, encf, vrow, P1, P2, R1, R2, GQ, GE, GK1, GK2, IDG,
    rankf, KT, VT, XC, XE, PB, RX, YX, SC, QB, ACC, MX, LS, STREAM, MID,
    loc_sem, ws, wr, os_, or_, os2, or2, fs, fr, p1s, p1r, p2s, p2r,
    ids_s, ids_r, q_s, q_r, e_s, e_r, k1_s, k1_r, k2_s, k2_r,
    xcs, xcr, xes, xer, rss, rsr, ags, agr,
):
    s = lax.axis_index("section")
    seq = lax.axis_index("seq")
    m = lax.axis_index("mp")
    y = seq // 8
    z = seq % 8
    partner = {"section": 1 - s}

    def zdev(k):
        return {"seq": y * 8 + (z + k) % 8}

    def ydev(k):
        return {"seq": ((y + k) % 8) * 8 + z}

    def xdev(k):
        return {"mp": (m + k) % 4}

    def remote(src, dst, send, recv, device):
        return pltpu.make_async_remote_copy(
            src_ref=src, dst_ref=dst, send_sem=send, recv_sem=recv, device_id=device, device_id_type=MESH
        )

    def ring(n):
        def run(f):
            lax.fori_loop(1, n, lambda k, c: (f(k), c)[1], 0)

        return run

    def far_first(n):
        def run(f):
            lax.fori_loop(
                0, n - 1, lambda j, c: (f(n // 2 + ((j + 1) // 2) * (1 - 2 * (j % 2))), c)[1], 0
            )

        return run

    groups = []

    class Group:
        def __init__(self, copy, n, slot, ref, recv):
            self.copy, self.n, self.slot, self.ref, self.sem = copy, n, slot, ref, recv
            self.waited = self.gone = False
            groups.append(self)
            far_first(n)(lambda k: copy(k).start())

        def wait_one(self, k):
            there = self.ref.at[self.slot(k)]
            remote(there, there, self.sem.at[k], self.sem.at[k], partner).wait_recv()

        def wait(self):
            self.waited = True
            ring(self.n)(self.wait_one)

        def left(self):
            if not self.gone:
                self.gone = True
                ring(self.n)(lambda k: self.copy(k).wait_send())

    class Single:
        def __init__(self, copy):
            self.copy = copy
            self.waited = False
            groups.append(self)
            copy.start()

        def wait(self):
            self.waited = True
            self.copy.wait_recv()

        def left(self):
            self.copy.wait_send()

    class Local:
        def __init__(self, copy):
            self.copy = copy
            self.waited = False
            groups.append(self)
            copy.start()

        def wait(self):
            self.waited = True
            self.copy.wait()

        def left(self):
            pass

    def finish():
        for g in groups:
            if not g.waited:
                g.wait()
            g.left()

    def from_z(k):
        return (z + 8 - k) % 8

    def from_y(k):
        return (y + 8 - k) % 8

    def from_x(k):
        return (m + 4 - k) % 4

    def halves(ref_out, ref_in, i):
        return pltpu.make_async_copy(ref_in, ref_out.at[s], loc_sem.at[i])

    barrier = pltpu.get_barrier_semaphore()
    def greet(device):
        pl.semaphore_signal(barrier, inc=1, device_id=device, device_id_type=MESH)

    far_first(8)(lambda k: (greet(zdev(k)), greet(ydev(k))))
    far_first(4)(lambda k: greet(xdev(k)))
    greet(partner)

    small = [
        pltpu.make_async_copy(src, dst, loc_sem.at[6 + i])
        for i, (src, dst) in enumerate(
            ((enc_h, enc), (ct3_h, ct3), (enc_gh, enc_g), (mask_h, mask_t), (attn_h, attn_g), (mlp_h, mlp_g))
        )
    ]
    for copy in small:
        copy.start()
    local = [
        Local(copy)
        for copy in (
            halves(E2, embed_w, 0), halves(W2, qkv_w, 1), halves(U2, up_w, 2), halves(D2, down_w, 3),
            pltpu.make_async_copy(out_w.at[pl.ds(HD, 128)], OA.at[s, m], loc_sem.at[4]),
            pltpu.make_async_copy(out_w.at[pl.ds(0, HD)], OB.at[s, m], loc_sem.at[5]),
        )
    ]

    for copy in small:
        copy.wait()
    mask_row = mask_t[...].astype(F32).reshape(1, WIDTH)
    attn_gain = attn_g[...].astype(F32).reshape(1, WIDTH)
    mlp_gain = mlp_g[...].astype(F32).reshape(1, WIDTH)
    enc_gain = jnp.concatenate(
        [enc_g[0:WIDTH].astype(F32).reshape(1, WIDTH), enc_g[WIDTH:ENC].astype(F32).reshape(1, WIDTH)], axis=1
    )
    table = ct3[...]
    vrow[...] = jnp.full((8, 128), -1.0, F32)
    vrow[0:1, 0:VIS_DEV] = vis[...].astype(F32)
    vids = vrow[0:1, :]
    vcol = jnp.sum(
        jnp.where(iota((16, 128), 1) == iota((16, 128), 0), jnp.broadcast_to(vids, (16, 128)), 0.0),
        axis=1, keepdims=True,
    )
    vis_code = nn(one_hot_rows(jnp.maximum(vcol, 0.0), 192), table)
    encf[...] = jnp.zeros((16, ENC), F32)
    encf[0:VIS_DEV, :] = enc[0].astype(F32)
    normed = (norm(encf[...]) * enc_gain).astype(BF16)

    own2[...] = jnp.full((72, 128), -1, jnp.int32)
    for i in range(8):
        own2[i * 8 : (i + 1) * 8, :] = owner[i * 1024 : (i + 1) * 1024].reshape(8, 128)
    for i in range(64, 67):
        own2[i : i + 1, :] = owner[i * 128 : (i + 1) * 128].reshape(1, 128)
    own2[67:68, 0:64] = owner[67 * 128 : PATCHES].reshape(1, 64)
    flags = jnp.where(own2[...] == seq, 1.0, 0.0).astype(F32)
    flagb = flags.astype(BF16)
    upper = jnp.where(iota((128, 128), 0) <= iota((128, 128), 1), 1.0, 0.0).astype(BF16)
    lower = jnp.where(iota((72, 72), 1) < iota((72, 72), 0), 1.0, 0.0).astype(BF16)
    within = nn(flagb, upper)
    before = jnp.sum(nn(lower, flagb), axis=1, keepdims=True)
    rankf[...] = jnp.where(flags > 0.5, within + before - 1.0, -1.0)
    own_j = fiota((ROWS, 128), 0)
    lane_row = fiota((ROWS, 128), 1)

    def find(h, total):
        row = jnp.broadcast_to(rankf[pl.ds(h, 1), :], (ROWS, 128))
        return total + jnp.where(row == own_j, lane_row + (h * 128).astype(F32), 0.0)

    own_ids = jnp.sum(
        lax.fori_loop(0, 68, find, jnp.zeros((ROWS, 128), F32), unroll=4), axis=1, keepdims=True
    )
    pl.semaphore_wait(barrier, 18)

    def weight(i, src, dst):
        return Single(remote(src, dst.at[s], ws.at[i], wr.at[i], partner))

    g_embed = weight(0, embed_w, E2)
    g_qkv = weight(1, qkv_w, W2)

    def oa_copy(k):
        return remote(out_w.at[pl.ds(HD, 128)], OA.at[s, m], os_.at[k], or_.at[k], xdev(k))

    def ob_copy(k):
        return remote(out_w.at[pl.ds(0, HD)], OB.at[s, m], os2.at[k], or2.at[k], xdev(k))

    g_oa = Group(oa_copy, 4, lambda k: (s, from_x(k)), OA, or_)
    g_ob = Group(ob_copy, 4, lambda k: (s, from_x(k)), OB, or2)
    own_code = nn(one_hot_rows(own_ids, 192), table)

    row64 = iota((64, WIDTH), 0)
    lane64 = iota((64, WIDTH), 1)
    group = jnp.where(row64 < 8, 0, jnp.where(row64 < 16, 1, jnp.where(row64 < 24, 2, 3)))
    inside = (lane64 >= group * 192) & (lane64 < group * 192 + 192)
    mask_centred = mask_row - jnp.mean(mask_row, axis=-1, keepdims=True)
    code = table[0:64].astype(F32) + table[64:128].astype(F32) + table[128:192].astype(F32)
    block = jnp.where(inside, mask_centred + code, 0.0)
    block_sum = jnp.sum(block, axis=1, keepdims=True)
    block_mean = block_sum * (1.0 / 192.0)
    off = jnp.where(inside, block - block_mean, 0.0)
    spread = jnp.sum(off * off, axis=1, keepdims=True)
    scaled = (block - block_sum * (1.0 / 768.0)) * attn_gain
    scaled_hi = scaled.astype(BF16)
    scaled_lo = (scaled - scaled_hi.astype(F32)).astype(BF16)
    pieces = jnp.concatenate([scaled_hi, scaled_lo], axis=0)
    lane128 = iota((64, 128), 1)
    row128 = iota((64, 128), 0)
    group128 = jnp.where(row128 < 8, 0, jnp.where(row128 < 16, 1, jnp.where(row128 < 24, 2, 3)))
    stat = jnp.where(lane128 == group128, block_mean, 0.0) + jnp.where(lane128 == 4, spread, 0.0)
    stat_t = jnp.transpose(jnp.concatenate([stat, stat], axis=0))[0:16, :]

    local[0].wait()
    g_embed.wait()
    embedded = (nn(normed[:, 0:WIDTH], E2[0]) + nn(normed[:, WIDTH:ENC], E2[1])).astype(BF16)
    attn_vis = (norm(embedded.astype(F32) + vis_code) * attn_gain).astype(BF16)
    local[1].wait()
    g_qkv.wait()
    qk = nt(attn_vis[:, 0:384], W2[0, 0:384, :]) + nt(attn_vis[:, 384:768], W2[1, 0:384, :])
    kv = nt(attn_vis[:, 0:384], W2[0, LOCAL:576, :]) + nt(attn_vis[:, 384:768], W2[1, LOCAL:576, :])
    lane16 = iota((16, 384), 1)
    row16 = fiota((16, 1), 0)

    def pick(low, high, shift):
        return select(row16, jnp.where((row16 >= low) & (row16 < high), row16 + shift, -1.0), 16)

    first, second, third = pick(0, 6, 0), pick(0, 6, 6), pick(6, 12, -6)

    def pack(pair, keys_values):
        left = jnp.where(lane16 < LOCAL, pair, 0.0).astype(BF16)
        right = jnp.where(lane16 >= LOCAL, pltpu.roll(pair, LOCAL, 1), 0.0).astype(BF16)
        return nn(first, left) + nn(second, right) + nn(keys_values, kv.astype(BF16))

    vhi = jnp.floor((vids + 0.5) * (1.0 / 128.0))
    vlo = vids - 128.0 * vhi
    row_ids = iota((16, 128), 0)
    id_part = jnp.where(row_ids == 12, vhi, jnp.where(row_ids == 13, vlo, 0.0))
    id_part = jnp.concatenate([id_part, jnp.zeros((16, 256), F32)], axis=1)
    P1[...] = (pack(qk, third) + id_part).astype(BF16)
    quarter = pltpu.roll(embedded.astype(F32), (WIDTH - m * LOCAL) % WIDTH, 1)[:, 0:384]
    P2[...] = pack(quarter, pick(6, 12, 0)).astype(BF16)
    R1[z] = P1[...]
    R2[y] = P2[...]

    def p1_copy(k):
        return remote(P1, R1.at[z], p1s.at[k], p1r.at[k], zdev(k))

    def p2_copy(k):
        return remote(P2, R2.at[y], p2s.at[k], p2r.at[k], ydev(k))

    g_p1 = Group(p1_copy, 8, from_z, R1, p1r)
    g_p2 = Group(p2_copy, 8, from_y, R2, p2r)
    g_up = weight(2, up_w, U2)
    g_down = weight(3, down_w, D2)

    kv_w0, kv_w1 = W2[0, LOCAL:576, :], W2[1, LOCAL:576, :]
    proj = nt(kv_w0, pieces[:, 0:384]) + nt(kv_w1, pieces[:, 384:768])
    proj = proj + pltpu.roll(proj, 64, 1)
    proj_hi = proj.astype(BF16)
    lane_p = iota((384, 128), 1)
    kv_table = jnp.where(lane_p < 64, proj_hi.astype(F32), proj - proj_hi.astype(F32)).astype(BF16)
    stat_hi = stat_t.astype(BF16)
    stat_table = jnp.where(
        iota((16, 128), 1) < 64, stat_hi.astype(F32), stat_t - stat_hi.astype(F32)
    ).astype(BF16)
    big_table = jnp.concatenate([kv_table, stat_table], axis=0)

    stream0 = mask_row + own_code
    attn_own = (norm(stream0) * attn_gain).astype(BF16)
    q_masked = nt(attn_own[:, 0:384], W2[0, 0:256, :]) + nt(attn_own[:, 384:768], W2[1, 0:256, :])

    def build(c):
        width = 512
        start = pl.multiple_of(c * width, width)
        patch = (iota((1, width), 1) + start).astype(F32)
        c0, c1, c2, c3 = coordinates(patch)
        sub = fiota((64, width), 0)
        value = jnp.where(
            sub < 8, c0, jnp.where(sub < 16, c1 + 8, jnp.where(sub < 24, c2 + 16, c3 + 24))
        )
        hot = jnp.where(sub == value, 1.0, 0.0).astype(BF16)
        raw = nn(big_table, jnp.concatenate([hot, hot], axis=0))
        m0, m1, m2, m3 = raw[384:385], raw[385:386], raw[386:387], raw[387:388]
        mean = (m0 + m1 + m2 + m3) * 0.25
        between = (m0 - mean) ** 2 + (m1 - mean) ** 2 + (m2 - mean) ** 2 + (m3 - mean) ** 2
        scale = lax.rsqrt(raw[388:389] * (1.0 / 768.0) + between * 0.25 + 1e-06)
        KT[0:LOCAL, pl.ds(start, width)] = (raw[0:LOCAL] * scale).astype(BF16)
        VT[HD:256, pl.ds(start, width)] = (raw[LOCAL:384] * scale).astype(BF16)
        KT[LOCAL:256, pl.ds(start, width)] = jnp.zeros((64, width), BF16)
        VT[0:HD, pl.ds(start, width)] = jnp.zeros((64, width), BF16)

    lax.fori_loop(0, 6, lambda c, x: (build(c), x)[1], 0)

    g_p1.wait()
    g_p2.wait()
    col = fiota((112, 1), 0)
    small = jnp.where(col < 48, col, col - 48)
    src = jnp.floor((small + 0.5) * (1.0 / 6.0))
    src = 16.0 * src + (small - 6.0 * src) + jnp.where(col < 48, 0.0, 6.0)
    src = jnp.where(col < 96, src, jnp.where(col < 104, 16.0 * (col - 96) + 12, 16.0 * (col - 104) + 13))
    chooser = select(col, src, 128)
    got1 = nn(chooser, R1[...].reshape(128, 384))
    got2 = nn(chooser[0:96], R2[...].reshape(128, 384))
    GQ[y] = got1[0:48].astype(BF16)
    GK1[y] = got1[48:96].astype(BF16)
    IDG[y] = 128.0 * got1[96:104, 0:128] + got1[104:112, 0:128]
    GE[z] = got2[0:48].astype(BF16)
    GK2[z] = got2[48:96].astype(BF16)

    def over(n, ref, slot, source, send, recv, device):
        def copy(k):
            return remote(ref.at[slot], ref.at[slot], send.at[k], recv.at[k], device(k))

        return Group(copy, n, source, ref, recv)

    c_ids = over(8, IDG, y, from_y, ids_s, ids_r, ydev)
    c_q = over(8, GQ, y, from_y, q_s, q_r, ydev)
    c_e = over(8, GE, z, from_z, e_s, e_r, zdev)

    def build_some(low, high):
        lax.fori_loop(low, high, lambda c, x: (build(c), x)[1], 0)

    local[4].wait()
    local[5].wait()
    g_oa.wait()
    g_ob.wait()
    forward_a = Single(remote(OA.at[s], OA.at[s], fs.at[0], fr.at[0], partner))
    forward_b = Single(remote(OB.at[s], OB.at[s], fs.at[1], fr.at[1], partner))
    build_some(6, 13)
    c_k1 = over(8, GK1, y, from_y, k1_s, k1_r, ydev)
    c_k2 = over(8, GK2, z, from_z, k2_s, k2_r, zdev)
    build_some(13, 17)
    c_ids.wait()

    ids = IDG[...].reshape(64, 128)
    lane_i = fiota((64, 128), 1)
    source = fiota((64, 1), 0) + 1.0
    hots, where_d, where_i = [], [], []
    for i in range(VIS_DEV):
        one = ids[:, i : i + 1]
        high = jnp.floor((one + 0.5) * (1.0 / 128.0))
        low = one - 128.0 * high
        hots.append(jnp.where(lane_i == high, 1.0, 0.0))
        hot = jnp.where(lane_i == low, 1.0, 0.0)
        where_d.append((hot * source).astype(BF16))
        where_i.append((hot * float(i)).astype(BF16))
    hot_t = jnp.transpose(jnp.concatenate(hots, axis=0)).astype(BF16)
    found = nn(
        hot_t,
        jnp.concatenate(
            [jnp.concatenate(where_d, axis=0), jnp.concatenate(where_i, axis=0)], axis=1
        ),
    )
    seen = found[:, 0:128]
    patch2 = fiota((128, 128), 0) * 128.0 + fiota((128, 128), 1)
    bias = jnp.where((seen > 0.5) | (patch2 >= PATCHES), NEG, 0.0)
    sub16 = iota((16, 128), 0)
    for h in range(68):
        KT[LOCAL : LOCAL + 16, h * 128 : (h + 1) * 128] = jnp.where(
            sub16 == 0, jnp.broadcast_to(bias[h : h + 1, :], (16, 128)), 0.0
        ).astype(BF16)
    own_hi = jnp.floor((own_ids + 0.5) * (1.0 / 128.0))
    own_lo = own_ids - 128.0 * own_hi
    hit_hi = jnp.where(lane_row == own_hi, 1.0, 0.0).astype(BF16)
    hit_lo = lane_row == own_lo
    place = nn(hit_hi, found.astype(BF16))
    own_d = jnp.sum(jnp.where(hit_lo, place[:, 0:128], 0.0), axis=1, keepdims=True) - 1.0
    own_i = jnp.sum(jnp.where(hit_lo, place[:, 128:256], 0.0), axis=1, keepdims=True)
    is_vis = own_d > -0.5
    late = own_i > 5.5
    own_i6 = jnp.where(late, own_i - 6.0, own_i)
    own_y = jnp.floor((own_d + 0.5) * 0.125)
    own_z = own_d - 8.0 * own_y
    row_yz = own_y * 48.0 + own_z * 6.0 + own_i6
    row_zy = own_z * 48.0 + own_y * 6.0 + own_i6

    def choose(row, gathered):
        lane = fiota((ROWS, 384), 1)
        hit = jnp.where((lane == row) & is_vis, 1.0, 0.0)
        one = nn(jnp.where(late, 0.0, hit).astype(BF16), gathered)
        two = nn(jnp.where(late, hit, 0.0).astype(BF16), gathered)
        both = one + pltpu.roll(two, LOCAL, 1)
        return jnp.where(iota((ROWS, 256), 1) < LOCAL, both[:, 0:256], 0.0)

    c_q.wait()
    q_vis = choose(row_yz, GQ[...].reshape(384, 384))
    queries = jnp.where(is_vis, q_vis, q_masked).astype(BF16).astype(F32) * (HD ** -0.5)
    lane_q = iota((ROWS, 256), 1)
    for h in range(3):
        keep = (lane_q >= h * HD) & (lane_q < (h + 1) * HD)
        QB[h * ROWS : (h + 1) * ROWS, :] = jnp.where(
            keep, queries, jnp.where(lane_q == LOCAL, 1.0, 0.0)
        ).astype(BF16)

    c_e.wait()
    XE[m] = choose(row_zy, GE[...].reshape(384, 384)).astype(BF16)

    c_xe = over(4, XE, m, from_x, xes, xer, xdev)

    MX[...] = jnp.full((3 * ROWS, 128), NEG, F32)
    LS[...] = jnp.zeros((3 * ROWS, 128), F32)
    ACC[...] = jnp.zeros((3 * ROWS, 256), F32)

    def absorb(scores, width, product):
        peak_old = MX[...]
        peak = jnp.maximum(peak_old, jnp.max(scores, axis=1, keepdims=True))
        factor = jnp.exp(peak_old - peak)
        weights_ = jnp.exp(scores - peak[:, 0:1])
        total = weights_[:, 0:128]
        for t in range(1, width // 128):
            total = total + weights_[:, t * 128 : (t + 1) * 128]
        MX[...] = peak
        LS[...] = LS[...] * factor + total
        ACC[...] = ACC[...] * jnp.concatenate([factor, factor], axis=1) + product(weights_.astype(BF16))

    def masked(c, x):
        start = pl.multiple_of(c * CHUNK, 128)
        scores = nn(QB[...], KT[:, pl.ds(start, CHUNK)])
        absorb(scores, CHUNK, lambda w: nt(w, VT[:, pl.ds(start, CHUNK)]))
        return x

    lax.fori_loop(0, KEYS // CHUNK, masked, 0)

    c_k1.wait()
    c_k2.wait()
    q_only = jnp.where(iota((3 * ROWS, 256), 1) < LOCAL, QB[...].astype(F32), 0.0).astype(BF16)

    seen_rows = jnp.concatenate([GK1[...].reshape(384, 384), GK2[...].reshape(384, 384)], axis=0)
    absorb(nt(q_only, seen_rows[:, 0:256]), 768, lambda w: nn(w, seen_rows[:, 128:384]))

    context = jnp.zeros((ROWS, 256), F32)
    for h in range(3):
        keep = (lane_q >= (h + 1) * HD) & (lane_q < (h + 2) * HD)
        part = slice(h * ROWS, (h + 1) * ROWS)
        total = jnp.sum(LS[part, :], axis=1, keepdims=True)
        context = context + jnp.where(keep, ACC[part, :] / total, 0.0)
    head0 = context[:, 0:128]
    lane80 = iota((80, 128), 1)
    XC[m, 0:ROWS, :] = context[:, 128:256].astype(BF16)
    XC[m, ROWS:224, :] = jnp.where(lane80 < HD, pltpu.roll(head0[0:80], HD, 1), head0[64:ROWS]).astype(BF16)
    c_xc = over(4, XC, m, from_x, xcs, xcr, xdev)

    c_xe.wait()
    filled = jnp.zeros((ROWS, WIDTH), F32)
    for i in range(4):
        wide = jnp.concatenate([XE[i].astype(F32), jnp.zeros((ROWS, 512), F32)], axis=1)
        filled = filled + (pltpu.roll(wide, i * LOCAL, 1) if i else wide)
    stream = jnp.where(is_vis, filled, mask_row) + own_code
    STREAM[...] = stream

    local[2].wait()
    local[3].wait()
    g_up.wait()
    g_down.wait()
    forward_a.wait()
    forward_b.wait()
    c_xc.wait()
    pairs = jnp.concatenate([XC[i, 0:ROWS, :] for i in range(4)], axis=1)
    lows, highs = [], []
    for i in (0, 2):
        one, two = XC[i, ROWS:224, :].astype(F32), XC[i + 1, ROWS:224, :].astype(F32)
        lows.append(jnp.where(lane80 < HD, one, pltpu.roll(two, HD, 1)).astype(BF16))
        highs.append(jnp.where(lane80 < HD, pltpu.roll(one, HD, 1), two).astype(BF16))
    singles = jnp.concatenate(
        [jnp.concatenate(lows, axis=1), jnp.concatenate(highs, axis=1)], axis=0
    )
    for half in range(2):
        cols = slice(half * 384, (half + 1) * 384)
        most = STREAM[:, cols] + nn(pairs, OA[half].reshape(512, 384))
        rest = nn(singles, OB[half].reshape(256, 384))
        MID[0:80, cols] = most[0:80] + rest[0:80]
        MID[80:ROWS, cols] = most[80:ROWS] + rest[96:160]

    mlp_in = (norm(MID[...]) * mlp_gain).astype(BF16)
    raised = nn(mlp_in[:, 0:384], U2[0]) + nn(mlp_in[:, 384:768], U2[1])
    hidden = (0.5 * raised * (1.0 + lax.erf(raised * np.float32(np.sqrt(0.5))))).astype(BF16)
    for half in range(2):
        PB[half] = nn(hidden, D2[half]).astype(BF16)

    def quadrant(q):
        return PB.at[q % 2, pl.ds(pl.multiple_of((q // 2) * 64, 16), 80)]

    def rs_copy(k):
        return remote(quadrant((m + k) % 4), RX.at[m], rss.at[k], rsr.at[k], xdev(k))

    c_rs = Group(rs_copy, 4, from_x, RX, rsr)
    RX[m] = PB[m % 2, pl.ds(pl.multiple_of((m // 2) * 64, 16), 80), :]
    c_rs.wait()
    YX[m] = (
        RX[0].astype(F32) + RX[1].astype(F32) + RX[2].astype(F32) + RX[3].astype(F32)
    ).astype(BF16)
    c_ag = over(4, YX, m, from_x, ags, agr, xdev)
    c_ag.wait()
    for half in range(2):
        cols = slice(half * 384, (half + 1) * 384)
        result[0:80, cols] = MID[0:80, cols] + YX[half].astype(F32)
        result[80:OWN, cols] = MID[80:OWN, cols] + YX[2 + half].astype(F32)[16:71]

    finish()


def shards(
    enc_rows, vis_index, owner_of, enc_gain, embed_weight, mask_token, attn_gain, qkv_weight,
    out_weight, mlp_gain, up_weight, down_weight,
):
    qkv_t = jnp.transpose(qkv_weight, (1, 2, 0)).reshape(576, 384)
    vm = pl.BlockSpec(memory_space=pltpu.VMEM)
    hbm = pl.BlockSpec(memory_space=pl.ANY)
    dma = pltpu.SemaphoreType.DMA
    V = pltpu.VMEM
    scratch = [
        V((2, 768, 768), BF16), V((2, 576, 384), BF16), V((2, 4, 128, 384), BF16), V((2, 4, 64, 384), BF16),
        V((2, 384, 768), BF16), V((2, 768, 384), BF16), V((72, 128), jnp.int32),
        V((1, VIS_DEV, ENC), BF16), V((ENC,), BF16), V((WIDTH,), BF16), V((WIDTH,), BF16), V((WIDTH,), BF16),
        V((192, WIDTH), BF16),
        V((16, ENC), F32), V((8, 128), F32), V((16, 384), BF16), V((16, 384), BF16),
        V((8, 16, 384), BF16), V((8, 16, 384), BF16),
        V((8, 48, 384), BF16), V((8, 48, 384), BF16), V((8, 48, 384), BF16), V((8, 48, 384), BF16),
        V((8, 8, 128), F32), V((72, 128), F32),
        V((256, KEYS), BF16), V((256, KEYS), BF16),
        V((4, 224, 128), BF16), V((4, ROWS, 256), BF16),
        V((2, ROWS, 384), BF16), V((4, 80, 384), BF16), V((4, 80, 384), BF16),
        V((8, 128), F32), V((3 * ROWS, 256), BF16), V((3 * ROWS, 256), F32),
        V((3 * ROWS, 128), F32), V((3 * ROWS, 128), F32), V((ROWS, WIDTH), F32), V((ROWS, WIDTH), F32),
        dma((12,)), dma((4,)), dma((4,)), dma((4,)), dma((4,)), dma((4,)), dma((4,)), dma((2,)), dma((2,)),
    ] + [dma((8,))] * 14 + [dma((4,))] * 8
    decoded = pl.pallas_call(
        kernel,
        out_shape=jax.ShapeDtypeStruct((OWN, WIDTH), F32),
        in_specs=[hbm, vm, vm] + [hbm] * 5 + [hbm, hbm, hbm, hbm, hbm],
        out_specs=vm,
        scratch_shapes=scratch,
        compiler_params=pltpu.CompilerParams(
            collective_id=0, has_side_effects=True, vmem_limit_bytes=56 * 1024 * 1024
        ),
        cost_estimate=pl.CostEstimate(flops=6_000_000_000, bytes_accessed=5_000_000, transcendentals=4_000_000),
    )(
        enc_rows, vis_index, owner_of, enc_gain, mask_token, attn_gain, mlp_gain, jnp.asarray(code_table()),
        embed_weight, qkv_t, out_weight, up_weight, down_weight,
    )
    return decoded[None]


def solution(mesh):
    in_specs = (
        P("section", "seq", None),
        P("section", "seq"),
        P(),
        P(),
        P("section", None),
        P(),
        P(),
        P("section", None, "mp"),
        P("mp", "section"),
        P(),
        P("section", "mp"),
        P("mp", "section"),
    )
    out_specs = P("section", "seq", None)
    return jax.shard_map(shards, mesh=mesh, in_specs=in_specs, out_specs=out_specs, check_vma=False)
```

```python
import functools

import jax
import jax.numpy as jnp
import numpy as np
from jax import lax
from jax.experimental import pallas as pl
from jax.experimental.pallas import tpu as pltpu
from jax.sharding import PartitionSpec as P

MESH = pl.DeviceIdType.MESH
F32 = jnp.float32
BF16 = jnp.bfloat16
GX = 6
PATCHES = 8640
OWN = 135
ROWS = 144
VIS_DEV = 12
WIDTH = 768
ENC = 1536
LOCAL = 192
HD = 64
NEG = -1e30
KEYS = 8704
CHUNK = 2176


def code_table():
    half = WIDTH // 8
    frequency = (1.0 / 10000.0 ** (np.arange(half, dtype=np.float32) / half)).astype(np.float32)
    table = np.zeros((64, WIDTH), np.float32)
    for c, (base, count) in enumerate(((0, GX), (8, GX), (16, GX), (24, 40))):
        angle = np.arange(count, dtype=np.float32)[:, None] * frequency[None, :]
        table[base : base + count, c * 192 : c * 192 + half] = np.sin(angle)
        table[base : base + count, c * 192 + half : (c + 1) * 192] = np.cos(angle)
    pieces = []
    for _ in range(3):
        piece = table.astype(BF16)
        pieces.append(piece)
        table = table - piece.astype(np.float32)
    return np.concatenate(pieces, axis=0)


def iota(shape, axis):
    return lax.broadcasted_iota(jnp.int32, shape, axis)


def fiota(shape, axis):
    return iota(shape, axis).astype(F32)


def nn(a, b):
    return lax.dot_general(a, b, (((1,), (0,)), ((), ())), preferred_element_type=F32)


def nt(a, b):
    return lax.dot_general(a, b, (((1,), (1,)), ((), ())), preferred_element_type=F32)


def coordinates(patch):
    c3 = jnp.floor((patch + 0.5) * (1.0 / 216.0))
    rest = patch - 216.0 * c3
    c2 = jnp.floor((rest + 0.5) * (1.0 / 36.0))
    rest = rest - 36.0 * c2
    c1 = jnp.floor((rest + 0.5) * (1.0 / 6.0))
    return rest - 6.0 * c1, c1, c2, c3


def one_hot_rows(patch, lanes):
    c0, c1, c2, c3 = coordinates(patch)
    lane = (iota((patch.shape[0], lanes), 1) & 63).astype(F32)
    value = jnp.where(
        lane < 8, c0, jnp.where(lane < 16, c1 + 8, jnp.where(lane < 24, c2 + 16, c3 + 24))
    )
    return jnp.where(lane == value, 1.0, 0.0).astype(BF16)


def norm(values):
    centred = values - jnp.mean(values, axis=-1, keepdims=True)
    spread = jnp.mean(centred * centred, axis=-1, keepdims=True)
    return centred * lax.rsqrt(spread + 1e-06)


def select(target, source, count):
    lane = fiota((target.shape[0], count), 1)
    return jnp.where(lane == source, 1.0, 0.0).astype(BF16)


def kernel(
    enc_h, vis, owner, enc_gh, mask_h, attn_h, mlp_h, ct3_h, embed_w, qkv_w, out_w, up_w, down_w,
    result,
    E2, W2, OA, OB, U2, D2, own2, enc, enc_g, mask_t, attn_g, mlp_g, ct3, encf, vrow, P1, P2, R1, R2, GQ, GE, GK1, GK2, IDG,
    rankf, KT, VT, XC, XE, PB, RX, YX, SC, QB, ACC, MX, LS, STREAM, MID,
    loc_sem, ws, wr, os_, or_, os2, or2, fs, fr, p1s, p1r, p2s, p2r,
    ids_s, ids_r, q_s, q_r, e_s, e_r, k1_s, k1_r, k2_s, k2_r,
    xcs, xcr, xes, xer, rss, rsr, ags, agr,
):
    s = lax.axis_index("section")
    seq = lax.axis_index("seq")
    m = lax.axis_index("mp")
    y = seq // 8
    z = seq % 8
    partner = {"section": 1 - s}

    def zdev(k):
        return {"seq": y * 8 + (z + k) % 8}

    def ydev(k):
        return {"seq": ((y + k) % 8) * 8 + z}

    def xdev(k):
        return {"mp": (m + k) % 4}

    def remote(src, dst, send, recv, device):
        return pltpu.make_async_remote_copy(
            src_ref=src, dst_ref=dst, send_sem=send, recv_sem=recv, device_id=device, device_id_type=MESH
        )

    def ring(n):
        def run(f):
            lax.fori_loop(1, n, lambda k, c: (f(k), c)[1], 0)

        return run

    def far_first(n):
        def run(f):
            lax.fori_loop(
                0, n - 1, lambda j, c: (f(n // 2 + ((j + 1) // 2) * (1 - 2 * (j % 2))), c)[1], 0
            )

        return run

    groups = []

    class Group:
        def __init__(self, copy, n, slot, ref, recv, now=True):
            self.copy, self.n, self.slot, self.ref, self.sem = copy, n, slot, ref, recv
            self.waited = self.gone = False
            groups.append(self)
            if now:
                far_first(n)(lambda k: copy(k).start())

        def wait_one(self, k):
            there = self.ref.at[self.slot(k)]
            remote(there, there, self.sem.at[k], self.sem.at[k], partner).wait_recv()

        def wait(self):
            self.waited = True
            ring(self.n)(self.wait_one)

        def left(self):
            if not self.gone:
                self.gone = True
                ring(self.n)(lambda k: self.copy(k).wait_send())

    class Single:
        def __init__(self, copy):
            self.copy = copy
            self.waited = False
            groups.append(self)
            copy.start()

        def wait(self):
            self.waited = True
            self.copy.wait_recv()

        def left(self):
            self.copy.wait_send()

    class Local:
        def __init__(self, copy):
            self.copy = copy
            self.waited = False
            groups.append(self)
            copy.start()

        def wait(self):
            self.waited = True
            self.copy.wait()

        def left(self):
            pass

    def finish():
        for g in groups:
            if not g.waited:
                g.wait()
            g.left()

    def from_z(k):
        return (z + 8 - k) % 8

    def from_y(k):
        return (y + 8 - k) % 8

    def from_x(k):
        return (m + 4 - k) % 4

    def halves(ref_out, ref_in, i):
        return pltpu.make_async_copy(ref_in, ref_out.at[s], loc_sem.at[i])

    barrier = pltpu.get_barrier_semaphore()
    def greet(device):
        pl.semaphore_signal(barrier, inc=1, device_id=device, device_id_type=MESH)

    far_first(8)(lambda k: (greet(zdev(k)), greet(ydev(k))))
    far_first(4)(lambda k: greet(xdev(k)))
    greet(partner)

    small = [
        pltpu.make_async_copy(src, dst, loc_sem.at[6 + i])
        for i, (src, dst) in enumerate(
            ((enc_h, enc), (ct3_h, ct3), (enc_gh, enc_g), (mask_h, mask_t), (attn_h, attn_g), (mlp_h, mlp_g))
        )
    ]
    for copy in small:
        copy.start()
    local = [
        Local(copy)
        for copy in (
            halves(E2, embed_w, 0), halves(W2, qkv_w, 1), halves(U2, up_w, 2), halves(D2, down_w, 3),
            pltpu.make_async_copy(out_w.at[pl.ds(HD, 128)], OA.at[s, m], loc_sem.at[4]),
            pltpu.make_async_copy(out_w.at[pl.ds(0, HD)], OB.at[s, m], loc_sem.at[5]),
        )
    ]

    for copy in small:
        copy.wait()
    mask_row = mask_t[...].astype(F32).reshape(1, WIDTH)
    attn_gain = attn_g[...].astype(F32).reshape(1, WIDTH)
    mlp_gain = mlp_g[...].astype(F32).reshape(1, WIDTH)
    enc_gain = jnp.concatenate(
        [enc_g[0:WIDTH].astype(F32).reshape(1, WIDTH), enc_g[WIDTH:ENC].astype(F32).reshape(1, WIDTH)], axis=1
    )
    table = ct3[...]
    vrow[...] = jnp.full((8, 128), -1.0, F32)
    vrow[0:1, 0:VIS_DEV] = vis[...].astype(F32)
    vids = vrow[0:1, :]
    vcol = jnp.sum(
        jnp.where(iota((16, 128), 1) == iota((16, 128), 0), jnp.broadcast_to(vids, (16, 128)), 0.0),
        axis=1, keepdims=True,
    )
    vis_code = nn(one_hot_rows(jnp.maximum(vcol, 0.0), 192), table)
    encf[...] = jnp.zeros((16, ENC), F32)
    encf[0:VIS_DEV, :] = enc[0].astype(F32)
    normed = (norm(encf[...]) * enc_gain).astype(BF16)

    own2[...] = jnp.full((72, 128), -1, jnp.int32)
    for i in range(8):
        own2[i * 8 : (i + 1) * 8, :] = owner[i * 1024 : (i + 1) * 1024].reshape(8, 128)
    for i in range(64, 67):
        own2[i : i + 1, :] = owner[i * 128 : (i + 1) * 128].reshape(1, 128)
    own2[67:68, 0:64] = owner[67 * 128 : PATCHES].reshape(1, 64)
    flags = jnp.where(own2[...] == seq, 1.0, 0.0).astype(F32)
    flagb = flags.astype(BF16)
    upper = jnp.where(iota((128, 128), 0) <= iota((128, 128), 1), 1.0, 0.0).astype(BF16)
    lower = jnp.where(iota((72, 72), 1) < iota((72, 72), 0), 1.0, 0.0).astype(BF16)
    within = nn(flagb, upper)
    before = jnp.sum(nn(lower, flagb), axis=1, keepdims=True)
    rankf[...] = jnp.where(flags > 0.5, within + before - 1.0, -1.0)
    own_j = fiota((ROWS, 128), 0)
    lane_row = fiota((ROWS, 128), 1)

    def find(h, total):
        row = jnp.broadcast_to(rankf[pl.ds(h, 1), :], (ROWS, 128))
        return total + jnp.where(row == own_j, lane_row + (h * 128).astype(F32), 0.0)

    own_ids = jnp.sum(
        lax.fori_loop(0, 68, find, jnp.zeros((ROWS, 128), F32), unroll=4), axis=1, keepdims=True
    )
    pl.semaphore_wait(barrier, 18)

    def weight(i, src, dst):
        return Single(remote(src, dst.at[s], ws.at[i], wr.at[i], partner))

    g_embed = weight(0, embed_w, E2)
    g_qkv = weight(1, qkv_w, W2)

    def oa_copy(k):
        return remote(out_w.at[pl.ds(HD, 128)], OA.at[s, m], os_.at[k], or_.at[k], xdev(k))

    def ob_copy(k):
        return remote(out_w.at[pl.ds(0, HD)], OB.at[s, m], os2.at[k], or2.at[k], xdev(k))

    g_oa = Group(oa_copy, 4, lambda k: (s, from_x(k)), OA, or_)
    g_ob = Group(ob_copy, 4, lambda k: (s, from_x(k)), OB, or2)
    own_code = nn(one_hot_rows(own_ids, 192), table)

    row64 = iota((64, WIDTH), 0)
    lane64 = iota((64, WIDTH), 1)
    group = jnp.where(row64 < 8, 0, jnp.where(row64 < 16, 1, jnp.where(row64 < 24, 2, 3)))
    inside = (lane64 >= group * 192) & (lane64 < group * 192 + 192)
    mask_centred = mask_row - jnp.mean(mask_row, axis=-1, keepdims=True)
    code = table[0:64].astype(F32) + table[64:128].astype(F32) + table[128:192].astype(F32)
    block = jnp.where(inside, mask_centred + code, 0.0)
    block_sum = jnp.sum(block, axis=1, keepdims=True)
    block_mean = block_sum * (1.0 / 192.0)
    off = jnp.where(inside, block - block_mean, 0.0)
    spread = jnp.sum(off * off, axis=1, keepdims=True)
    scaled = (block - block_sum * (1.0 / 768.0)) * attn_gain
    scaled_hi = scaled.astype(BF16)
    scaled_lo = (scaled - scaled_hi.astype(F32)).astype(BF16)
    pieces = jnp.concatenate([scaled_hi, scaled_lo], axis=0)
    lane128 = iota((64, 128), 1)
    row128 = iota((64, 128), 0)
    group128 = jnp.where(row128 < 8, 0, jnp.where(row128 < 16, 1, jnp.where(row128 < 24, 2, 3)))
    stat = jnp.where(lane128 == group128, block_mean, 0.0) + jnp.where(lane128 == 4, spread, 0.0)
    stat_t = jnp.transpose(jnp.concatenate([stat, stat], axis=0))[0:16, :]

    local[0].wait()
    g_embed.wait()
    embedded = (nn(normed[:, 0:WIDTH], E2[0]) + nn(normed[:, WIDTH:ENC], E2[1])).astype(BF16)
    attn_vis = (norm(embedded.astype(F32) + vis_code) * attn_gain).astype(BF16)
    local[1].wait()
    g_qkv.wait()
    qk = nt(attn_vis[:, 0:384], W2[0, 0:384, :]) + nt(attn_vis[:, 384:768], W2[1, 0:384, :])
    kv = nt(attn_vis[:, 0:384], W2[0, LOCAL:576, :]) + nt(attn_vis[:, 384:768], W2[1, LOCAL:576, :])
    lane16 = iota((16, 384), 1)
    row16 = fiota((16, 1), 0)

    def pick(low, high, shift):
        return select(row16, jnp.where((row16 >= low) & (row16 < high), row16 + shift, -1.0), 16)

    first, second, third = pick(0, 6, 0), pick(0, 6, 6), pick(6, 12, -6)

    def pack(pair, keys_values):
        left = jnp.where(lane16 < LOCAL, pair, 0.0).astype(BF16)
        right = jnp.where(lane16 >= LOCAL, pltpu.roll(pair, LOCAL, 1), 0.0).astype(BF16)
        return nn(first, left) + nn(second, right) + nn(keys_values, kv.astype(BF16))

    vhi = jnp.floor((vids + 0.5) * (1.0 / 128.0))
    vlo = vids - 128.0 * vhi
    row_ids = iota((16, 128), 0)
    id_part = jnp.where(row_ids == 12, vhi, jnp.where(row_ids == 13, vlo, 0.0))
    id_part = jnp.concatenate([id_part, jnp.zeros((16, 256), F32)], axis=1)
    P1[...] = (pack(qk, third) + id_part).astype(BF16)
    quarter = pltpu.roll(embedded.astype(F32), (WIDTH - m * LOCAL) % WIDTH, 1)[:, 0:384]
    P2[...] = pack(quarter, pick(6, 12, 0)).astype(BF16)
    R1[z] = P1[...]
    R2[y] = P2[...]

    def p1_copy(k):
        return remote(P1, R1.at[z], p1s.at[k], p1r.at[k], zdev(k))

    def p2_copy(k):
        return remote(P2, R2.at[y], p2s.at[k], p2r.at[k], ydev(k))

    g_p1 = Group(p1_copy, 8, from_z, R1, p1r)
    g_p2 = Group(p2_copy, 8, from_y, R2, p2r)
    g_up = weight(2, up_w, U2)
    g_down = weight(3, down_w, D2)

    kv_w0, kv_w1 = W2[0, LOCAL:576, :], W2[1, LOCAL:576, :]
    proj = nt(kv_w0, pieces[:, 0:384]) + nt(kv_w1, pieces[:, 384:768])
    proj = proj + pltpu.roll(proj, 64, 1)
    proj_hi = proj.astype(BF16)
    lane_p = iota((384, 128), 1)
    kv_table = jnp.where(lane_p < 64, proj_hi.astype(F32), proj - proj_hi.astype(F32)).astype(BF16)
    stat_hi = stat_t.astype(BF16)
    stat_table = jnp.where(
        iota((16, 128), 1) < 64, stat_hi.astype(F32), stat_t - stat_hi.astype(F32)
    ).astype(BF16)
    big_table = jnp.concatenate([kv_table, stat_table], axis=0)

    stream0 = mask_row + own_code
    attn_own = (norm(stream0) * attn_gain).astype(BF16)
    q_masked = nt(attn_own[:, 0:384], W2[0, 0:256, :]) + nt(attn_own[:, 384:768], W2[1, 0:256, :])

    def build(c):
        width = 512
        start = pl.multiple_of(c * width, width)
        patch = (iota((1, width), 1) + start).astype(F32)
        c0, c1, c2, c3 = coordinates(patch)
        sub = fiota((64, width), 0)
        value = jnp.where(
            sub < 8, c0, jnp.where(sub < 16, c1 + 8, jnp.where(sub < 24, c2 + 16, c3 + 24))
        )
        hot = jnp.where(sub == value, 1.0, 0.0).astype(BF16)
        raw = nn(big_table, jnp.concatenate([hot, hot], axis=0))
        m0, m1, m2, m3 = raw[384:385], raw[385:386], raw[386:387], raw[387:388]
        mean = (m0 + m1 + m2 + m3) * 0.25
        between = (m0 - mean) ** 2 + (m1 - mean) ** 2 + (m2 - mean) ** 2 + (m3 - mean) ** 2
        scale = lax.rsqrt(raw[388:389] * (1.0 / 768.0) + between * 0.25 + 1e-06)
        KT[0:LOCAL, pl.ds(start, width)] = (raw[0:LOCAL] * scale).astype(BF16)
        VT[HD:256, pl.ds(start, width)] = (raw[LOCAL:384] * scale).astype(BF16)
        KT[LOCAL:256, pl.ds(start, width)] = jnp.zeros((64, width), BF16)
        VT[0:HD, pl.ds(start, width)] = jnp.zeros((64, width), BF16)

    lax.fori_loop(0, 6, lambda c, x: (build(c), x)[1], 0)

    g_p1.wait()
    col = fiota((112, 1), 0)
    small = jnp.where(col < 48, col, col - 48)
    src = jnp.floor((small + 0.5) * (1.0 / 6.0))
    src = 16.0 * src + (small - 6.0 * src) + jnp.where(col < 48, 0.0, 6.0)
    src = jnp.where(col < 96, src, jnp.where(col < 104, 16.0 * (col - 96) + 12, 16.0 * (col - 104) + 13))
    chooser = select(col, src, 128)
    got1 = nn(chooser, R1[...].reshape(128, 384))
    GQ[y] = got1[0:48].astype(BF16)
    GK1[y] = got1[48:96].astype(BF16)
    IDG[y] = 128.0 * got1[96:104, 0:128] + got1[104:112, 0:128]

    def over(n, ref, slot, source, send, recv, device):
        def copy(k):
            return remote(ref.at[slot], ref.at[slot], send.at[k], recv.at[k], device(k))

        return Group(copy, n, source, ref, recv)

    c_ids = over(8, IDG, y, from_y, ids_s, ids_r, ydev)
    c_q = over(8, GQ, y, from_y, q_s, q_r, ydev)
    g_p2.wait()
    got2 = nn(chooser[0:96], R2[...].reshape(128, 384))
    GE[z] = got2[0:48].astype(BF16)
    GK2[z] = got2[48:96].astype(BF16)
    c_e = over(8, GE, z, from_z, e_s, e_r, zdev)

    def build_some(low, high):
        lax.fori_loop(low, high, lambda c, x: (build(c), x)[1], 0)

    local[4].wait()
    local[5].wait()
    g_oa.wait()
    g_ob.wait()
    forward_a = Single(remote(OA.at[s], OA.at[s], fs.at[0], fr.at[0], partner))
    forward_b = Single(remote(OB.at[s], OB.at[s], fs.at[1], fr.at[1], partner))
    build_some(6, 13)
    c_k1 = over(8, GK1, y, from_y, k1_s, k1_r, ydev)
    c_k2 = over(8, GK2, z, from_z, k2_s, k2_r, zdev)
    build_some(13, 17)
    c_ids.wait()

    ids = IDG[...].reshape(64, 128)
    lane_i = fiota((64, 128), 1)
    source = fiota((64, 1), 0) + 1.0
    hots, where_d, where_i = [], [], []
    for i in range(VIS_DEV):
        one = ids[:, i : i + 1]
        high = jnp.floor((one + 0.5) * (1.0 / 128.0))
        low = one - 128.0 * high
        hots.append(jnp.where(lane_i == high, 1.0, 0.0))
        hot = jnp.where(lane_i == low, 1.0, 0.0)
        where_d.append((hot * source).astype(BF16))
        where_i.append((hot * float(i)).astype(BF16))
    hot_t = jnp.transpose(jnp.concatenate(hots, axis=0)).astype(BF16)
    found = nn(
        hot_t,
        jnp.concatenate(
            [jnp.concatenate(where_d, axis=0), jnp.concatenate(where_i, axis=0)], axis=1
        ),
    )
    seen = found[:, 0:128]
    patch2 = fiota((128, 128), 0) * 128.0 + fiota((128, 128), 1)
    bias = jnp.where((seen > 0.5) | (patch2 >= PATCHES), NEG, 0.0)
    sub16 = iota((16, 128), 0)
    for h in range(68):
        KT[LOCAL : LOCAL + 16, h * 128 : (h + 1) * 128] = jnp.where(
            sub16 == 0, jnp.broadcast_to(bias[h : h + 1, :], (16, 128)), 0.0
        ).astype(BF16)
    own_hi = jnp.floor((own_ids + 0.5) * (1.0 / 128.0))
    own_lo = own_ids - 128.0 * own_hi
    hit_hi = jnp.where(lane_row == own_hi, 1.0, 0.0).astype(BF16)
    hit_lo = lane_row == own_lo
    place = nn(hit_hi, found.astype(BF16))
    own_d = jnp.sum(jnp.where(hit_lo, place[:, 0:128], 0.0), axis=1, keepdims=True) - 1.0
    own_i = jnp.sum(jnp.where(hit_lo, place[:, 128:256], 0.0), axis=1, keepdims=True)
    is_vis = own_d > -0.5
    late = own_i > 5.5
    own_i6 = jnp.where(late, own_i - 6.0, own_i)
    own_y = jnp.floor((own_d + 0.5) * 0.125)
    own_z = own_d - 8.0 * own_y
    row_yz = own_y * 48.0 + own_z * 6.0 + own_i6
    row_zy = own_z * 48.0 + own_y * 6.0 + own_i6

    def choose(row, gathered):
        lane = fiota((ROWS, 384), 1)
        hit = jnp.where((lane == row) & is_vis, 1.0, 0.0)
        one = nn(jnp.where(late, 0.0, hit).astype(BF16), gathered)
        two = nn(jnp.where(late, hit, 0.0).astype(BF16), gathered)
        both = one + pltpu.roll(two, LOCAL, 1)
        return jnp.where(iota((ROWS, 256), 1) < LOCAL, both[:, 0:256], 0.0)

    c_q.wait()
    q_vis = choose(row_yz, GQ[...].reshape(384, 384))
    queries = jnp.where(is_vis, q_vis, q_masked).astype(BF16).astype(F32) * (HD ** -0.5)
    lane_q = iota((ROWS, 256), 1)
    for h in range(3):
        keep = (lane_q >= h * HD) & (lane_q < (h + 1) * HD)
        QB[h * ROWS : (h + 1) * ROWS, :] = jnp.where(
            keep, queries, jnp.where(lane_q == LOCAL, 1.0, 0.0)
        ).astype(BF16)

    c_e.wait()
    XE[m] = choose(row_zy, GE[...].reshape(384, 384)).astype(BF16)

    c_xe = over(4, XE, m, from_x, xes, xer, xdev)

    MX[...] = jnp.full((3 * ROWS, 128), NEG, F32)
    LS[...] = jnp.zeros((3 * ROWS, 128), F32)
    ACC[...] = jnp.zeros((3 * ROWS, 256), F32)

    def absorb(scores, width, product):
        peak_old = MX[...]
        peak = jnp.maximum(peak_old, jnp.max(scores, axis=1, keepdims=True))
        factor = jnp.exp(peak_old - peak)
        weights_ = jnp.exp(scores - peak[:, 0:1])
        total = weights_[:, 0:128]
        for t in range(1, width // 128):
            total = total + weights_[:, t * 128 : (t + 1) * 128]
        MX[...] = peak
        LS[...] = LS[...] * factor + total
        ACC[...] = ACC[...] * jnp.concatenate([factor, factor], axis=1) + product(weights_.astype(BF16))

    def masked(c, x):
        start = pl.multiple_of(c * CHUNK, 128)
        scores = nn(QB[...], KT[:, pl.ds(start, CHUNK)])
        absorb(scores, CHUNK, lambda w: nt(w, VT[:, pl.ds(start, CHUNK)]))
        return x

    lax.fori_loop(0, KEYS // CHUNK, masked, 0)

    c_k1.wait()
    c_k2.wait()
    q_only = jnp.where(iota((3 * ROWS, 256), 1) < LOCAL, QB[...].astype(F32), 0.0).astype(BF16)

    seen_rows = jnp.concatenate([GK1[...].reshape(384, 384), GK2[...].reshape(384, 384)], axis=0)
    absorb(nt(q_only, seen_rows[:, 0:256]), 768, lambda w: nn(w, seen_rows[:, 128:384]))

    context = jnp.zeros((ROWS, 256), F32)
    for h in range(3):
        keep = (lane_q >= (h + 1) * HD) & (lane_q < (h + 2) * HD)
        part = slice(h * ROWS, (h + 1) * ROWS)
        total = jnp.sum(LS[part, :], axis=1, keepdims=True)
        context = context + jnp.where(keep, ACC[part, :] / total, 0.0)
    head0 = context[:, 0:128]
    lane80 = iota((80, 128), 1)
    XC[m, 0:ROWS, :] = context[:, 128:256].astype(BF16)
    XC[m, ROWS:224, :] = jnp.where(lane80 < HD, pltpu.roll(head0[0:80], HD, 1), head0[64:ROWS]).astype(BF16)
    c_xc = over(4, XC, m, from_x, xcs, xcr, xdev)

    c_xe.wait()
    filled = jnp.zeros((ROWS, WIDTH), F32)
    for i in range(4):
        wide = jnp.concatenate([XE[i].astype(F32), jnp.zeros((ROWS, 512), F32)], axis=1)
        filled = filled + (pltpu.roll(wide, i * LOCAL, 1) if i else wide)
    stream = jnp.where(is_vis, filled, mask_row) + own_code
    STREAM[...] = stream

    local[2].wait()
    local[3].wait()
    g_up.wait()
    g_down.wait()
    forward_a.wait()
    forward_b.wait()
    c_xc.wait()
    pairs = jnp.concatenate([XC[i, 0:ROWS, :] for i in range(4)], axis=1)
    lows, highs = [], []
    for i in (0, 2):
        one, two = XC[i, ROWS:224, :].astype(F32), XC[i + 1, ROWS:224, :].astype(F32)
        lows.append(jnp.where(lane80 < HD, one, pltpu.roll(two, HD, 1)).astype(BF16))
        highs.append(jnp.where(lane80 < HD, pltpu.roll(one, HD, 1), two).astype(BF16))
    singles = jnp.concatenate(
        [jnp.concatenate(lows, axis=1), jnp.concatenate(highs, axis=1)], axis=0
    )
    for half in range(2):
        cols = slice(half * 384, (half + 1) * 384)
        most = STREAM[:, cols] + nn(pairs, OA[half].reshape(512, 384))
        rest = nn(singles, OB[half].reshape(256, 384))
        MID[0:80, cols] = most[0:80] + rest[0:80]
        MID[80:ROWS, cols] = most[80:ROWS] + rest[96:160]

    mlp_in = (norm(MID[...]) * mlp_gain).astype(BF16)
    raised = nn(mlp_in[:, 0:384], U2[0]) + nn(mlp_in[:, 384:768], U2[1])
    hidden = (0.5 * raised * (1.0 + lax.erf(raised * np.float32(np.sqrt(0.5))))).astype(BF16)
    def quadrant(q):
        return PB.at[q % 2, pl.ds(pl.multiple_of((q // 2) * 64, 16), 80)]

    def rs_copy(k):
        return remote(quadrant((m + k) % 4), RX.at[m], rss.at[k], rsr.at[k], xdev(k))

    c_rs = Group(rs_copy, 4, from_x, RX, rsr, now=False)
    for half in range(2):
        PB[half] = nn(hidden, D2[half]).astype(BF16)

        def send(k, half=half):
            pl.when((m + k) % 2 == half)(lambda: rs_copy(k).start())

        far_first(4)(send)
    RX[m] = PB[m % 2, pl.ds(pl.multiple_of((m // 2) * 64, 16), 80), :]
    c_rs.wait()
    YX[m] = (
        RX[0].astype(F32) + RX[1].astype(F32) + RX[2].astype(F32) + RX[3].astype(F32)
    ).astype(BF16)
    c_ag = over(4, YX, m, from_x, ags, agr, xdev)
    c_ag.wait()
    for half in range(2):
        cols = slice(half * 384, (half + 1) * 384)
        result[0:80, cols] = MID[0:80, cols] + YX[half].astype(F32)
        result[80:OWN, cols] = MID[80:OWN, cols] + YX[2 + half].astype(F32)[16:71]

    finish()


def shards(
    enc_rows, vis_index, owner_of, enc_gain, embed_weight, mask_token, attn_gain, qkv_weight,
    out_weight, mlp_gain, up_weight, down_weight,
):
    qkv_t = jnp.transpose(qkv_weight, (1, 2, 0)).reshape(576, 384)
    vm = pl.BlockSpec(memory_space=pltpu.VMEM)
    hbm = pl.BlockSpec(memory_space=pl.ANY)
    dma = pltpu.SemaphoreType.DMA
    V = pltpu.VMEM
    scratch = [
        V((2, 768, 768), BF16), V((2, 576, 384), BF16), V((2, 4, 128, 384), BF16), V((2, 4, 64, 384), BF16),
        V((2, 384, 768), BF16), V((2, 768, 384), BF16), V((72, 128), jnp.int32),
        V((1, VIS_DEV, ENC), BF16), V((ENC,), BF16), V((WIDTH,), BF16), V((WIDTH,), BF16), V((WIDTH,), BF16),
        V((192, WIDTH), BF16),
        V((16, ENC), F32), V((8, 128), F32), V((16, 384), BF16), V((16, 384), BF16),
        V((8, 16, 384), BF16), V((8, 16, 384), BF16),
        V((8, 48, 384), BF16), V((8, 48, 384), BF16), V((8, 48, 384), BF16), V((8, 48, 384), BF16),
        V((8, 8, 128), F32), V((72, 128), F32),
        V((256, KEYS), BF16), V((256, KEYS), BF16),
        V((4, 224, 128), BF16), V((4, ROWS, 256), BF16),
        V((2, ROWS, 384), BF16), V((4, 80, 384), BF16), V((4, 80, 384), BF16),
        V((8, 128), F32), V((3 * ROWS, 256), BF16), V((3 * ROWS, 256), F32),
        V((3 * ROWS, 128), F32), V((3 * ROWS, 128), F32), V((ROWS, WIDTH), F32), V((ROWS, WIDTH), F32),
        dma((12,)), dma((4,)), dma((4,)), dma((4,)), dma((4,)), dma((4,)), dma((4,)), dma((2,)), dma((2,)),
    ] + [dma((8,))] * 14 + [dma((4,))] * 8
    decoded = pl.pallas_call(
        kernel,
        out_shape=jax.ShapeDtypeStruct((OWN, WIDTH), F32),
        in_specs=[hbm, vm, vm] + [hbm] * 5 + [hbm, hbm, hbm, hbm, hbm],
        out_specs=vm,
        scratch_shapes=scratch,
        compiler_params=pltpu.CompilerParams(
            collective_id=0, has_side_effects=True, vmem_limit_bytes=56 * 1024 * 1024
        ),
        cost_estimate=pl.CostEstimate(flops=6_000_000_000, bytes_accessed=5_000_000, transcendentals=4_000_000),
    )(
        enc_rows, vis_index, owner_of, enc_gain, mask_token, attn_gain, mlp_gain, jnp.asarray(code_table()),
        embed_weight, qkv_t, out_weight, up_weight, down_weight,
    )
    return decoded[None]


def solution(mesh):
    in_specs = (
        P("section", "seq", None),
        P("section", "seq"),
        P(),
        P(),
        P("section", None),
        P(),
        P(),
        P("section", None, "mp"),
        P("mp", "section"),
        P(),
        P("section", "mp"),
        P("mp", "section"),
    )
    out_specs = P("section", "seq", None)
    return jax.shard_map(shards, mesh=mesh, in_specs=in_specs, out_specs=out_specs, check_vma=False)
```
